512 devices in a mesh: dp: 64 (over z, y_lo, core), mp: 8 (over y_hi, x).
Axes of the slice: x: 4, y: 8 (y_hi: 2, y_lo: 4; y = y_hi * 4 + y_lo), z: 8, core: 2. Of those that a mesh axis runs over, the one named last changes fastest.
Arguments:
- residual: bfloat16 [16384, 4608], P('dp', 'mp'), may hold values from -6 to 6
- out_grad: bfloat16 [16384, 4608], P('dp', 'mp'), may hold values from -6 to 6
- ffn_weights: bfloat16 [3, 256, 4608], P(None, 'mp'), may hold values from -0.09375 to 0.09375
- norm_gain: float32 [4608], replicated, may hold values from 0.1 to 1.9
- exponents: int32 [3], replicated, may hold values from 3 to 6, as said below
- sign_bits: int32 [4608], replicated, may hold values from 0 to 1
Outputs:
- resid_grad: bfloat16 [16384, 4608], P('dp', 'mp')
- weight_grads: bfloat16 [3, 256, 4608], P(None, 'mp')
The draws below stay inside these ranges and needn't reach their ends.
Inputs may be any that keep to these rules, and one draw needn't show every extreme that they name: `exponents`: one exponent for each of the gate, up and down gradients; every draw holds both 3 and 6. `sign_bits`: one bit per feature.
All inputs are finite; a program needn't handle non-finite values.
Results may differ from the reference program's by a relative error of at most 0.01.
Values may be sent and summed in bfloat16 or wider, within the bound.
No kernel may reach another device: no remote copies, remote signals or barrier semaphores. Data moves between devices by JAX's collectives and lax.ppermute only.
A program may use at most 64 MiB of HBM per device.

```python
import math
import jax
import jax.numpy as jnp
from jax import lax

D = 4608
TOK_DEV = 256
BUCKET_DEV = 32
TOKENS = 16384
BUCKET = 256
N_DP = 64
N_MP = 8


def draw_exponents(key, part):
    key = jax.random.fold_in(key, 11)
    third = jax.random.randint(jax.random.fold_in(key, 1), (1,), 3, 7, dtype=jnp.int32)
    values = jnp.concatenate([jnp.array([3, 6], dtype=jnp.int32), third])
    order = jax.random.permutation(jax.random.fold_in(key, 2), jnp.arange(3, dtype=jnp.int32))
    return values[order].astype(jnp.int32)


def place_ends(drawn, rng, smallest, largest):
    longest = drawn.shape.index(max(drawn.shape))
    spots = []
    for shift in (0, 1):
        where = [jax.random.randint(jax.random.fold_in(rng, axis), (), 0, length) for axis, length in enumerate(drawn.shape)]
        where[longest] = (where[longest] + shift) % drawn.shape[longest]
        spots.append(tuple(where))
    return drawn.at[spots[0]].set(smallest).at[spots[1]].set(largest)


def block_scale(key, extent, cuts, least, high):
    def one(axis_at, blocks):
        steps = jax.random.uniform(jax.random.fold_in(jax.random.fold_in(key, 6), axis_at), (blocks,), jnp.float32, least / len(cuts), high / len(cuts))
        return jnp.repeat(jnp.exp(steps), extent[axis_at] // blocks).reshape((-1,) + (1,) * (len(extent) - axis_at - 1))

    level = one(*cuts[0])
    for cut in cuts[1:]:
        level = level * one(*cut)
    return level


def scatter_about(own_key, shape, width, limit, split=(), kind=jnp.bfloat16):
    values = width * jax.random.normal(own_key, shape, jnp.float32)
    if split:
        values = values * block_scale(own_key, shape, split, -0.22, 0.18)
    return jnp.clip(values, -limit, limit).astype(kind)


def setup_inputs(seed: int = 0) -> dict:
    key_list = jax.random.split(jax.random.key(seed), 7)
    residual = scatter_about(key_list[0], (TOKENS, D), 1.0, 6.0, ((0, 64), (1, 8)))
    out_grad = scatter_about(key_list[1], (TOKENS, D), 1.0, 6.0, ((0, 64), (1, 8)))
    ffn_weights = scatter_about(key_list[2], (3, BUCKET, D), D ** -0.5, 0.09375, ((1, 8),))
    norm_gain = jnp.clip(1.0 + 0.18 * jax.random.normal(key_list[3], (D,), jnp.float32), 0.1, 1.9)
    exponents = draw_exponents(jax.random.fold_in(key_list[6], 71), 0)
    sign_bits = place_ends(jax.random.randint(key_list[5], (D,), 0, 2), jax.random.fold_in(key_list[5], 1), 0, 1).astype(jnp.int32)
    return dict(residual=residual, out_grad=out_grad, ffn_weights=ffn_weights, norm_gain=norm_gain, exponents=exponents, sign_bits=sign_bits)


def hadamard():
    indices = jnp.arange(128, dtype=jnp.int32)
    anded = jnp.bitwise_and(indices[:, None], indices[None, :])
    parity = jnp.zeros((128, 128), jnp.int32)
    for offset in range(7):
        parity = parity + jnp.bitwise_and(jnp.right_shift(anded, offset), 1)
    return (1 - 2 * (parity % 2)).astype(jnp.float32) / math.sqrt(128.0)

def gelu_parts(values):
    tanh_input = 0.7978845608 * (values + 0.044715 * values * values * values)
    tanhed = jnp.tanh(tanh_input)
    forward = 0.5 * values * (1.0 + tanhed)
    gelu_slope = 0.5 * (1.0 + tanhed) + 0.5 * values * (1.0 - tanhed * tanhed) * 0.7978845608 * (1.0 + 3.0 * 0.044715 * values * values)
    return (forward, gelu_slope)

def reference(residual, out_grad, ffn_weights, norm_gain, exponents, sign_bits):
    hadamard_table = hadamard()
    sign_table = (2 * sign_bits - 1).astype(jnp.float32).reshape(D // 128, 128)
    scales = jnp.exp2(exponents.astype(jnp.float32))
    grouped = ffn_weights.astype(jnp.float32).reshape(3, N_MP, BUCKET_DEV, D)

    def one_group(running, pieces):
        full_rows, grads_in = pieces
        rows_wide = full_rows.astype(jnp.float32)
        inverse = lax.rsqrt(lax.optimization_barrier(jnp.mean(rows_wide * rows_wide, axis=1, keepdims=True)) + 1e-06)
        unit_rows = rows_wide * inverse
        normed = (unit_rows * norm_gain).astype(jnp.bfloat16)
        gate_pre = jnp.dot(normed, ffn_weights[0].T, preferred_element_type=jnp.float32)
        up_proj = jnp.dot(normed, ffn_weights[1].T, preferred_element_type=jnp.float32)
        activated, gelu_slope = gelu_parts(gate_pre)
        hidden = (activated * up_proj).astype(jnp.bfloat16)
        hidden_grad = jnp.dot(grads_in, ffn_weights[2].T, preferred_element_type=jnp.float32)
        gate_grad = (hidden_grad * up_proj * gelu_slope).astype(jnp.bfloat16)
        up_grad = (hidden_grad * activated).astype(jnp.bfloat16)
        gate_split = gate_grad.astype(jnp.float32).reshape(-1, N_MP, BUCKET_DEV)
        up_split = up_grad.astype(jnp.float32).reshape(-1, N_MP, BUCKET_DEV)
        terms = jnp.einsum('tgh,ghd->gtd', gate_split, grouped[0]) + jnp.einsum('tgh,ghd->gtd', up_split, grouped[1])
        rounded = lax.optimization_barrier(terms.astype(jnp.bfloat16))
        normed_grad = lax.optimization_barrier(jnp.sum(rounded.astype(jnp.float32), axis=0))
        feature_grad = normed_grad * norm_gain
        row_mean = lax.optimization_barrier(jnp.mean(feature_grad * unit_rows, axis=1, keepdims=True))
        resid_grad = (grads_in.astype(jnp.float32) + inverse * (feature_grad - unit_rows * row_mean)).astype(jnp.bfloat16)
        gate_wgrad = jnp.dot(gate_grad.T, normed, preferred_element_type=jnp.float32)
        up_wgrad = jnp.dot(up_grad.T, normed, preferred_element_type=jnp.float32)
        down_wgrad = jnp.dot(hidden.T, grads_in, preferred_element_type=jnp.float32)
        stacked = jnp.stack([gate_wgrad, up_wgrad, down_wgrad]).reshape(3, BUCKET, D // 128, 128) * sign_table
        rotated = jnp.einsum('kubj,jc->kubc', stacked, hadamard_table, precision=lax.Precision.HIGHEST)
        quantized = jnp.clip(rotated * scales[:, None, None, None], -127.0, 127.0).astype(jnp.bfloat16)
        quantized = lax.optimization_barrier(quantized)
        return (running + quantized.astype(jnp.float32), resid_grad)
    start_sum = jnp.zeros((3, BUCKET, D // 128, 128), jnp.float32)
    grouped_rows = residual.reshape(N_DP, TOK_DEV, D)
    grouped_grads = out_grad.reshape(N_DP, TOK_DEV, D)
    running, resid_grads = lax.scan(one_group, start_sum, (grouped_rows, grouped_grads))
    summed = lax.optimization_barrier(running.astype(jnp.bfloat16)).astype(jnp.float32)
    factors = jnp.exp2(-exponents.astype(jnp.float32)) / N_DP
    restored = jnp.einsum('kubj,jc->kubc', summed * factors[:, None, None, None], hadamard_table, precision=lax.Precision.HIGHEST) * sign_table
    return (resid_grads.reshape(TOKENS, D), restored.astype(jnp.bfloat16).reshape(3, BUCKET, D))
```

```python
import functools

import jax
import jax.numpy as jnp
import numpy as np
from jax import lax
from jax.experimental import pallas as pl
from jax.experimental.pallas import tpu as pltpu
from jax.sharding import Mesh
from jax.sharding import PartitionSpec as P

F32 = jnp.float32
BF16 = jnp.bfloat16
DP = ("z", "yl", "c")
MP = ("yh", "x")
VMEM_LIMIT = 40 * 1024 * 1024
FEATURES = 4608
CONTRACT_LAST = (((1,), (1,)), ((), ()))
CONTRACT_FIRST = (((0,), (0,)), ((), ()))


def signed_hadamard():
    table = np.array([[1.0]], np.float32)
    for _ in range(7):
        table = np.block([[table, table], [table, -table]])
    return table


def gelu_parts(values):
    tanh_input = 0.7978845608 * (values + 0.044715 * values * values * values)
    tanhed = jnp.tanh(tanh_input)
    forward = 0.5 * values * (1.0 + tanhed)
    gelu_slope = 0.5 * (1.0 + tanhed) + 0.5 * values * (1.0 - tanhed * tanhed) * 0.7978845608 * (
        1.0 + 3.0 * 0.044715 * values * values
    )
    return (forward, gelu_slope)


def pieces(values):
    high = values.astype(BF16)
    rest = values - high.astype(F32)
    middle = rest.astype(BF16)
    low = (rest - middle.astype(F32)).astype(BF16)
    return (high, middle, low)


def dot(left, right, dims=(((1,), (0,)), ((), ()))):
    return lax.dot_general(left, right, dims, preferred_element_type=F32)


def places():
    odd = lax.axis_index("x") % 2
    pair = lax.axis_index("yh") * 2 + lax.axis_index("x") // 2
    return (lax.axis_index("c"), odd, pair * 9)


def local_rows(table_ref, first, odd):
    rows = [table_ref[pl.ds(first + 5 * odd + b, 1), :] for b in range(4)]
    return jnp.concatenate(rows + [table_ref[pl.ds(first + 4, 1), :]], axis=1)


def forward_kernel(recv_ref, both_ref, x_ref, xh_ref, g_ref, gh_ref, gain_ref, part_ref, w_ref, inv_ref):
    core, odd, first = places()
    for near in range(2):
        side = core if near == 0 else 1 - core
        for j in range(8):
            for b in range(5):
                for k in range(3):
                    w_ref[pl.ds(k * 256 + near * 128 + j * 16, 16), pl.ds(b * 128, 128)] = both_ref[
                        side, j, pl.ds(b * 48 + k * 16, 16), :
                    ]
    sums = jnp.sum(recv_ref[:, 240:256, :].astype(F32), axis=0)
    total = sums[0:2] + sums[2:4] + sums[4:6]
    diagonal = lax.broadcasted_iota(jnp.int32, (128, 128), 0) == lax.broadcasted_iota(jnp.int32, (128, 128), 1)
    columns = [
        jnp.sum(jnp.where(diagonal, total[i : i + 1], 0.0), axis=1, keepdims=True) for i in range(2)
    ]
    inverse = lax.rsqrt(jnp.concatenate(columns, axis=0) / FEATURES + 1e-06)
    inv_ref[...] = jnp.broadcast_to(inverse, (256, 128))
    gain = local_rows(gain_ref, first, odd)
    own_half = (lax.broadcasted_iota(jnp.int32, (256, 128), 1) >= 64) == (odd == 1)

    def widened(main_ref, half_ref):
        half = jnp.where(own_half, half_ref[...].astype(F32), 0.0)
        return jnp.concatenate([main_ref[...].astype(F32), half], axis=1)

    normed = (widened(x_ref, xh_ref) * inverse * gain).astype(BF16)
    grads = widened(g_ref, gh_ref).astype(BF16)
    part_ref[:, 0:512] = dot(normed, w_ref[0:512], CONTRACT_LAST).astype(BF16)
    part_ref[:, 512:768] = dot(grads, w_ref[512:768], CONTRACT_LAST).astype(BF16)


def activation_kernel(parts_ref, out_ref):
    total = parts_ref[0].astype(F32)
    for i in range(1, 8):
        total = total + parts_ref[i].astype(F32)
    gate_pre, up_proj, hidden_grad = total[:, 0:256], total[:, 256:512], total[:, 512:768]
    activated, slope = gelu_parts(gate_pre)
    hidden = (activated * up_proj).astype(BF16)
    gate_grad = (hidden_grad * up_proj * slope).astype(BF16)
    up_grad = (hidden_grad * activated).astype(BF16)
    products = gate_grad.astype(F32) * gate_pre + up_grad.astype(F32) * up_proj
    row_mean = jnp.sum(products, axis=1, keepdims=True) / FEATURES
    high, middle, low = pieces(jnp.broadcast_to(row_mean, (32, 128)))
    lane = lax.broadcasted_iota(jnp.int32, (32, 128), 1)
    tail = jnp.where(lane == 0, high.astype(F32), jnp.where(lane == 1, middle.astype(F32), low.astype(F32)))
    tail = jnp.where(lane < 3, tail, 0.0).astype(BF16)
    message = jnp.concatenate([gate_grad, up_grad, hidden, tail], axis=1)
    for i in range(8):
        out_ref[i] = message


def gradient_kernel(
    acts_ref, w_ref, x_ref, xh_ref, g_ref, gh_ref, inv_ref, gain_ref, sign_ref, table_ref, exps_ref, resid_ref, keep_ref, send_ref
):
    _, odd, first = places()
    gain = local_rows(gain_ref, first, odd)
    sign = (2 * local_rows(sign_ref, first, odd) - 1).astype(F32)
    inverse = inv_ref[:, 0:1]
    acts = acts_ref[...].reshape(256, 896)
    gate_grad, up_grad, hidden = acts[:, 0:256], acts[:, 256:512], acts[:, 512:768]
    row_mean = jnp.sum(acts[:, 768:896].astype(F32), axis=1, keepdims=True)
    unit = jnp.concatenate([x_ref[...], xh_ref[...]], axis=1).astype(F32) * inverse
    grads = jnp.concatenate([g_ref[...], gh_ref[...]], axis=1)
    normed = (unit * gain).astype(BF16)
    normed_grad = dot(gate_grad, w_ref[0:256]) + dot(up_grad, w_ref[256:512])
    resid = grads.astype(F32) + inverse * (normed_grad * gain - unit * row_mean)
    resid_ref[...] = resid.astype(BF16)
    table = table_ref[...]
    for k, (left, right) in enumerate(((gate_grad, normed), (up_grad, normed), (hidden, grads))):
        term = dot(left, right, CONTRACT_FIRST) * sign
        scale = jnp.left_shift(1, exps_ref[k]).astype(F32) * float(128.0**-0.5)
        for b in range(5):
            high, middle, low = pieces(term[:, b * 128 : (b + 1) * 128])
            rotated = (dot(low, table) + dot(middle, table)) + dot(high, table)
            values = jnp.clip(rotated * scale, -127.0, 127.0)
            for near, out_ref in enumerate((keep_ref, send_ref)):
                half = values[near * 128 : near * 128 + 128].reshape(8, 2, 8, 128)
                if b < 4:
                    out_ref[k * 8 + b] = half[:, 0].reshape(64, 128).astype(BF16)
                    out_ref[k * 8 + 4 + b] = half[:, 1].reshape(64, 128).astype(BF16)
                else:
                    chosen = jnp.where(odd == 1, half[:, 1], half[:, 0])
                    out_ref[24 + k] = chosen.reshape(64, 128).astype(BF16)
    for out_ref in (keep_ref, send_ref):
        for s in range(27, 32):
            out_ref[s] = jnp.zeros((64, 128), BF16)


def pair_kernel(keep_ref, other_ref, out_ref):
    out_ref[...] = (keep_ref[...].astype(F32) + other_ref[...].astype(F32)).astype(BF16)


def total_kernel(terms_ref, out_ref):
    total = terms_ref[0].astype(F32)
    for i in range(1, 32):
        total = total + terms_ref[i].astype(F32)
    rounded = total.astype(BF16)
    for i in range(32):
        out_ref[i] = rounded


def restore_kernel(share_ref, sign_ref, table_ref, exps_ref, out_ref):
    table = table_ref[...]
    for k in range(3):
        e = exps_ref[k]
        factor = jnp.where(e == 3, 2.0**-9, jnp.where(e == 4, 2.0**-10, jnp.where(e == 5, 2.0**-11, 2.0**-12)))
        factor = factor.astype(F32) * float(128.0**-0.5)
        for q in range(2):
            rows = pl.ds(16 * q, 16)

            def put(block, low_half, high_half):
                sign = (2 * sign_ref[block : block + 1, :] - 1).astype(F32) * factor
                both = jnp.concatenate([low_half, high_half], axis=0) * sign
                out_ref[k, rows, block * 128 : (block + 1) * 128] = both.astype(BF16)

            for b in range(4):
                halves = [dot(share_ref[q, k * 8 + 4 * i + b], table) for i in range(2)]
                for m in range(8):
                    put(
                        9 * (m // 2) + 5 * (m % 2) + b,
                        halves[0][m * 8 : m * 8 + 8],
                        halves[1][m * 8 : m * 8 + 8],
                    )
            shared = dot(share_ref[q, 24 + k], table)
            for p in range(4):
                put(9 * p + 4, shared[16 * p : 16 * p + 8], shared[16 * p + 8 : 16 * p + 16])


def call(kernel, outs, scalars=0):
    def run(*operands):
        count = len(operands)
        spaces = [pltpu.SMEM if i >= count - scalars else pltpu.VMEM for i in range(count)]
        return pl.pallas_call(
            kernel,
            out_shape=[jax.ShapeDtypeStruct(shape, dtype) for shape, dtype in outs],
            in_specs=[pl.BlockSpec(memory_space=space) for space in spaces],
            out_specs=[pl.BlockSpec(memory_space=pltpu.VMEM) for _ in outs],
            compiler_params=pltpu.CompilerParams(vmem_limit_bytes=VMEM_LIMIT),
            name=kernel.__name__,
        )(*operands)

    return run


def aligned(values, odd):
    return (
        jnp.where(odd == 1, values[:, 64:576], values[:, 0:512]),
        jnp.where(odd == 1, values[:, 0:64], values[:, 512:576]),
    )


def per_device(residual, out_grad, ffn_weights, norm_gain, exponents, sign_bits):
    core, odd, _ = places()
    x_main, x_half = aligned(residual, odd)
    g_main, g_half = aligned(out_grad, odd)
    swapped = lax.ppermute(
        jnp.concatenate([x_half, g_half], axis=1), "x", [(0, 1), (1, 0), (2, 3), (3, 2)]
    )

    def shared(own, other):
        return jnp.where(
            odd == 1, jnp.concatenate([other, own], axis=1), jnp.concatenate([own, other], axis=1)
        )

    x_shared = shared(x_half, swapped[:, 0:64])
    g_shared = shared(g_half, swapped[:, 64:128])

    wide = residual.astype(F32)
    squares = jnp.stack(pieces(jnp.sum(wide * wide, axis=1))).reshape(6, 128)
    squares = jnp.concatenate([squares, jnp.zeros((10, 128), BF16)], axis=0)
    mine = lax.dynamic_slice_in_dim(ffn_weights, core * 16, 16, 1).reshape(48, 36, 128)
    chunks = []
    for m in range(8):
        start = 9 * (m // 2)
        blocks = [start + 5 * (m % 2) + b for b in range(4)] + [start + 4]
        chunks.append(jnp.concatenate([mine[:, b] for b in blocks] + [squares], axis=0))
    received = lax.all_to_all(jnp.stack(chunks), MP, 0, 0)
    both = lax.all_gather(received, "c", axis=0)

    gain = norm_gain.reshape(36, 128)
    signs = sign_bits.reshape(36, 128)
    table = jnp.asarray(signed_hadamard(), BF16)
    parts, weights, inverse = call(
        forward_kernel, [((256, 768), BF16), ((768, 640), BF16), ((256, 128), F32)]
    )(received, both, x_main, x_shared, g_main, g_shared, gain)
    parts = lax.all_to_all(parts.reshape(8, 32, 768), MP, 0, 0)
    (message,) = call(activation_kernel, [((8, 32, 896), BF16)])(parts)
    acts = lax.all_to_all(message, MP, 0, 0)
    resid, keep, send = call(
        gradient_kernel,
        [((256, 640), BF16), ((32, 64, 128), BF16), ((32, 64, 128), BF16)],
        scalars=1,
    )(acts, weights, x_main, x_shared, g_main, g_shared, inverse, gain, signs, table, exponents)
    other = lax.ppermute(send, "c", [(0, 1), (1, 0)])
    (terms,) = call(pair_kernel, [((32, 64, 128), BF16)])(keep, other)
    terms = lax.all_to_all(terms, ("z", "yl"), 0, 0)
    (share,) = call(total_kernel, [((32, 64, 128), BF16)])(terms)
    gathered = lax.all_to_all(share.reshape(256, 8, 128), ("z", "yl", "yh", "x"), 0, 0)
    gathered = lax.all_gather(gathered, "c", axis=0).reshape(2, 32, 64, 128)
    (weight_grads,) = call(restore_kernel, [((3, 32, 4608), BF16)], scalars=1)(
        gathered, signs, table, exponents
    )
    resid_grad = jnp.where(
        odd == 1,
        jnp.concatenate([resid[:, 576:640], resid[:, 0:512]], axis=1),
        resid[:, 0:576],
    )
    return (resid_grad, weight_grads)


def solution(mesh):
    axes = ("z", "yl", "c", "yh", "x")
    fine = Mesh(mesh.devices.reshape(8, 4, 2, 2, 4), axes)
    rows = P(DP, MP)
    return jax.shard_map(
        per_device,
        mesh=fine,
        in_specs=(rows, rows, P(None, MP, None), P(), P(), P()),
        out_specs=(rows, P(None, MP, None)),
        check_vma=False,
    )
```

```python
import functools

import jax
import jax.numpy as jnp
import numpy as np
from jax import lax
from jax.experimental import pallas as pl
from jax.experimental.pallas import tpu as pltpu
from jax.sharding import Mesh
from jax.sharding import PartitionSpec as P

F32 = jnp.float32
BF16 = jnp.bfloat16
DP = ("z", "yl", "c")
MP = ("yh", "x")
VMEM_LIMIT = 40 * 1024 * 1024
FEATURES = 4608
CONTRACT_LAST = (((1,), (1,)), ((), ()))
CONTRACT_FIRST = (((0,), (0,)), ((), ()))


def signed_hadamard():
    table = np.array([[1.0]], np.float32)
    for _ in range(7):
        table = np.block([[table, table], [table, -table]])
    return table


def gelu_parts(values):
    tanh_input = 0.7978845608 * (values + 0.044715 * values * values * values)
    tanhed = jnp.tanh(tanh_input)
    forward = 0.5 * values * (1.0 + tanhed)
    gelu_slope = 0.5 * (1.0 + tanhed) + 0.5 * values * (1.0 - tanhed * tanhed) * 0.7978845608 * (
        1.0 + 3.0 * 0.044715 * values * values
    )
    return (forward, gelu_slope)


def pieces(values):
    high = values.astype(BF16)
    rest = values - high.astype(F32)
    middle = rest.astype(BF16)
    low = (rest - middle.astype(F32)).astype(BF16)
    return (high, middle, low)


def dot(left, right, dims=(((1,), (0,)), ((), ()))):
    return lax.dot_general(left, right, dims, preferred_element_type=F32)


def places():
    odd = lax.axis_index("x") % 2
    pair = lax.axis_index("yh") * 2 + lax.axis_index("x") // 2
    return (lax.axis_index("c"), odd, pair * 9)


def local_rows(table_ref, first, odd):
    rows = [table_ref[pl.ds(first + 5 * odd + b, 1), :] for b in range(4)]
    return jnp.concatenate(rows + [table_ref[pl.ds(first + 4, 1), :]], axis=1)


def prepare_kernel(x_ref, g_ref, w_ref, send_ref, half_ref):
    core, odd, _ = places()
    rows = pl.ds(pl.multiple_of(core * 16, 16), 16)
    for m in range(8):
        start = 9 * (m // 2)
        for b, block in enumerate([start + 5 * (m % 2) + b for b in range(4)] + [start + 4]):
            for k in range(3):
                send_ref[m, pl.ds(b * 48 + k * 16, 16), :] = w_ref[k, rows, block * 128 : (block + 1) * 128]
    halves = [
        jnp.where(odd == 1, ref[:, 0:64].astype(F32), ref[:, 512:576].astype(F32)) for ref in (x_ref, g_ref)
    ]
    half_ref[...] = jnp.concatenate(halves, axis=1).astype(BF16)


def aligned(ref, odd):
    values = ref[...].astype(F32)
    zeros = jnp.zeros((256, 64), F32)
    return jnp.where(
        odd == 1,
        jnp.concatenate([values[:, 64:576], zeros, values[:, 0:64]], axis=1),
        jnp.concatenate([values, zeros], axis=1),
    )


def forward_kernel(recv_ref, x_ref, g_ref, far_x_ref, far_g_ref, gain_ref, part_ref, w_ref, xa_ref, ga_ref):
    _, odd, first = places()
    for j in range(8):
        for b in range(5):
            for k in range(3):
                w_ref[k * 128 + j * 16 : k * 128 + j * 16 + 16, b * 128 : (b + 1) * 128] = recv_ref[
                    j, b * 48 + k * 16 : b * 48 + k * 16 + 16, :
                ]
    wide = jnp.concatenate([aligned(x_ref, odd), aligned(far_x_ref, odd)], axis=0)
    grads = jnp.concatenate([aligned(g_ref, odd), aligned(far_g_ref, odd)], axis=0).astype(BF16)
    xa_ref[...] = wide.astype(BF16)
    ga_ref[...] = grads
    gained = wide * local_rows(gain_ref, first, odd)
    high = gained.astype(BF16)
    low = (gained - high.astype(F32)).astype(BF16)
    pair = w_ref[0:256]
    gate_up = (dot(low, pair, CONTRACT_LAST) + dot(high, pair, CONTRACT_LAST)).astype(BF16)
    down = dot(grads, w_ref[256:384], CONTRACT_LAST).astype(BF16)
    squares = wide * wide
    ones = jnp.ones((8, 640), BF16)
    square_high = squares.astype(BF16)
    square_low = (squares - square_high.astype(F32)).astype(BF16)
    sums = dot(ones, square_low, CONTRACT_LAST) + dot(ones, square_high, CONTRACT_LAST)
    row = lax.broadcasted_iota(jnp.int32, (8, 256), 0)
    tail = jnp.zeros((8, 256), F32)
    for i, piece in enumerate(pieces(sums)):
        for side in range(2):
            tail = jnp.where(row == 2 * i + side, piece[:, side * 256 : side * 256 + 256].astype(F32), tail)
    tail = jnp.concatenate([tail, jnp.zeros((8, 128), F32)], axis=1)
    for i in range(8):
        near, far = slice(32 * i, 32 * i + 32), slice(256 + 32 * i, 256 + 32 * i + 32)
        part_ref[i, 0:32, 0:256] = gate_up[near]
        part_ref[i, 0:32, 256:384] = down[near]
        part_ref[i, 32:64, 0:256] = gate_up[far]
        part_ref[i, 32:64, 256:384] = down[far]
        part_ref[i, 64:72, :] = tail.astype(BF16)


def activation_kernel(parts_ref, out_ref, inv_ref):
    total = parts_ref[0].astype(F32)
    for i in range(1, 8):
        total = total + parts_ref[i].astype(F32)
    sums = total[64:72, 0:256]
    inverse_rows = lax.rsqrt((sums[0:2] + sums[2:4] + sums[4:6]) / FEATURES + 1e-06)
    inv_ref[0:2, :] = inverse_rows
    inv_ref[2:8, :] = jnp.zeros((6, 256), F32)
    mine = 32 * (lax.axis_index("yh") * 4 + lax.axis_index("x"))
    place = lax.broadcasted_iota(jnp.int32, (32, 256), 1) == lax.broadcasted_iota(jnp.int32, (32, 256), 0) + mine
    columns = [
        jnp.sum(jnp.where(place, inverse_rows[i : i + 1], 0.0), axis=1, keepdims=True) for i in range(2)
    ]
    inverse = jnp.concatenate(columns, axis=0)
    gate_pre, up_proj, hidden_grad = (
        total[0:64, 0:128] * inverse,
        total[0:64, 128:256] * inverse,
        total[0:64, 256:384],
    )
    activated, slope = gelu_parts(gate_pre)
    hidden = (activated * up_proj).astype(BF16)
    gate_grad = (hidden_grad * up_proj * slope).astype(BF16)
    up_grad = (hidden_grad * activated).astype(BF16)
    products = gate_grad.astype(F32) * gate_pre + up_grad.astype(F32) * up_proj
    row_mean = jnp.sum(products, axis=1, keepdims=True) / FEATURES
    diagonal = lax.broadcasted_iota(jnp.int32, (64, 128), 0) == lax.broadcasted_iota(jnp.int32, (64, 128), 1)
    mean_row = jnp.sum(jnp.where(diagonal, row_mean, 0.0), axis=0, keepdims=True)
    row = lax.broadcasted_iota(jnp.int32, (8, 128), 0)
    tail = jnp.zeros((8, 128), F32)
    for i, piece in enumerate(pieces(mean_row)):
        tail = jnp.where(row == i, piece.astype(F32), tail)
    tail = jnp.concatenate([tail, jnp.zeros((8, 256), F32)], axis=1).astype(BF16)
    acts = jnp.concatenate([gate_grad, up_grad, hidden], axis=1)
    for i in range(8):
        out_ref[i, 0:64, :] = acts
        out_ref[i, 64:72, :] = tail


def gradient_kernel(
    acts_ref, w_ref, xa_ref, ga_ref, near_half_ref, far_half_ref, inv_ref, gain_ref, sign_ref, table_ref, exps_ref,
    term_ref, near_ref, far_ref,
):
    _, odd, first = places()
    gain = local_rows(gain_ref, first, odd)
    sign = (2 * local_rows(sign_ref, first, odd) - 1).astype(F32)
    table = table_ref[...]
    lane = lax.broadcasted_iota(jnp.int32, (256, 128), 1)
    theirs = (lane >= 64) == (odd == 0)
    square = lax.broadcasted_iota(jnp.int32, (256, 256), 0) == lax.broadcasted_iota(jnp.int32, (256, 256), 1)
    diagonal = lax.broadcasted_iota(jnp.int32, (64, 128), 0) == lax.broadcasted_iota(jnp.int32, (64, 128), 1)
    means = []
    for i in range(8):
        tail = acts_ref[i, 64:72, 0:128].astype(F32)
        mean_row = tail[0:1] + tail[1:2] + tail[2:3]
        means.append(jnp.sum(jnp.where(diagonal, mean_row, 0.0), axis=1, keepdims=True))
    sides = []
    for side, half_ref in enumerate((near_half_ref, far_half_ref)):
        tokens = slice(side * 256, side * 256 + 256)
        inverse = jnp.sum(jnp.where(square, inv_ref[side : side + 1, :], 0.0), axis=1, keepdims=True)
        row_mean = jnp.concatenate([mean[side * 32 : side * 32 + 32] for mean in means], axis=0)
        acts = jnp.concatenate([acts_ref[i, side * 32 : side * 32 + 32, :] for i in range(8)], axis=0)
        halves = half_ref[...].astype(F32)
        turned = pltpu.roll(halves, 64, 1)
        x_half = jnp.where(theirs, jnp.where(odd == 1, halves, turned), xa_ref[tokens, 512:640].astype(F32))
        g_half = jnp.where(theirs, jnp.where(odd == 1, turned, halves), ga_ref[tokens, 512:640].astype(F32))
        unit = jnp.concatenate([xa_ref[tokens, 0:512].astype(F32), x_half], axis=1) * inverse
        grads = jnp.concatenate([ga_ref[tokens, 0:512], g_half.astype(BF16)], axis=1)
        normed = (unit * gain).astype(BF16)
        gate_grad, up_grad, hidden = acts[:, 0:128], acts[:, 128:256], acts[:, 256:384]
        normed_grad = dot(acts[:, 0:256], w_ref[0:256])
        resid = inverse * (normed_grad * gain - unit * row_mean)
        if side == 0:
            near_ref[...] = resid
        else:
            far_ref[...] = resid.astype(BF16)
        sides.append(((gate_grad, normed), (up_grad, normed), (hidden, grads)))
    for k in range(3):
        scale = jnp.left_shift(1, exps_ref[k]).astype(F32) * float(128.0**-0.5)
        terms = [dot(*sides[side][k], CONTRACT_FIRST) * sign for side in range(2)]
        for b in range(5):
            total = None
            for term in terms:
                high, middle, low = pieces(term[:, b * 128 : (b + 1) * 128])
                rotated = (dot(low, table) + dot(middle, table)) + dot(high, table)
                quantized = jnp.clip(rotated * scale, -127.0, 127.0).astype(BF16).astype(F32)
                total = quantized if total is None else total + quantized
            half = total.reshape(8, 2, 8, 128)
            if b < 4:
                term_ref[k * 8 + b] = half[:, 0].reshape(64, 128).astype(BF16)
                term_ref[k * 8 + 4 + b] = half[:, 1].reshape(64, 128).astype(BF16)
            else:
                chosen = jnp.where(odd == 1, half[:, 1], half[:, 0])
                term_ref[24 + k] = chosen.reshape(64, 128).astype(BF16)
    for s in range(27, 32):
        term_ref[s] = jnp.zeros((64, 128), BF16)


def resid_kernel(g_ref, near_ref, far_ref, out_ref):
    _, odd, _ = places()
    total = near_ref[...] + far_ref[...].astype(F32)
    own = jnp.where(
        odd == 1, jnp.concatenate([total[:, 576:640], total[:, 0:512]], axis=1), total[:, 0:576]
    )
    out_ref[...] = (g_ref[...].astype(F32) + own).astype(BF16)


def total_kernel(terms_ref, out_ref):
    total = terms_ref[0].astype(F32)
    for i in range(1, 32):
        total = total + terms_ref[i].astype(F32)
    rounded = total.astype(BF16)
    for i in range(32):
        out_ref[i] = rounded


def restore_kernel(near_ref, far_ref, sign_ref, table_ref, exps_ref, out_ref):
    table = table_ref[...]
    core, _, _ = places()
    for k in range(3):
        e = exps_ref[k]
        factor = jnp.where(e == 3, 2.0**-9, jnp.where(e == 4, 2.0**-10, jnp.where(e == 5, 2.0**-11, 2.0**-12)))
        factor = factor.astype(F32) * float(128.0**-0.5)
        for q, share_ref in ((core, near_ref), (1 - core, far_ref)):
            rows = pl.ds(pl.multiple_of(16 * q, 16), 16)

            def put(block, low_half, high_half):
                sign = (2 * sign_ref[block : block + 1, :] - 1).astype(F32) * factor
                both = jnp.concatenate([low_half, high_half], axis=0) * sign
                out_ref[k, rows, block * 128 : (block + 1) * 128] = both.astype(BF16)

            for b in range(4):
                halves = [dot(share_ref[k * 8 + 4 * i + b], table) for i in range(2)]
                for m in range(8):
                    put(
                        9 * (m // 2) + 5 * (m % 2) + b,
                        halves[0][m * 8 : m * 8 + 8],
                        halves[1][m * 8 : m * 8 + 8],
                    )
            shared = dot(share_ref[24 + k], table)
            for p in range(4):
                put(9 * p + 4, shared[16 * p : 16 * p + 8], shared[16 * p + 8 : 16 * p + 16])


def call(kernel, outs, scalars=0):
    def run(*operands):
        count = len(operands)
        spaces = [pltpu.SMEM if i >= count - scalars else pltpu.VMEM for i in range(count)]
        return pl.pallas_call(
            kernel,
            out_shape=[jax.ShapeDtypeStruct(shape, dtype) for shape, dtype in outs],
            in_specs=[pl.BlockSpec(memory_space=space) for space in spaces],
            out_specs=[pl.BlockSpec(memory_space=pltpu.VMEM) for _ in outs],
            compiler_params=pltpu.CompilerParams(vmem_limit_bytes=VMEM_LIMIT),
            name=kernel.__name__,
        )(*operands)

    return run


def per_device(residual, out_grad, ffn_weights, norm_gain, exponents, sign_bits):
    gain = norm_gain.reshape(36, 128)
    signs = sign_bits.reshape(36, 128)
    table = jnp.asarray(signed_hadamard(), BF16)
    cores = [(0, 1), (1, 0)]

    send, half = call(prepare_kernel, [((8, 240, 128), BF16), ((256, 128), BF16)])(residual, out_grad, ffn_weights)
    received = lax.all_to_all(send, MP, 0, 0)
    near_x, near_g, half = lax.optimization_barrier((residual, out_grad, half))
    far_x = lax.ppermute(near_x, "c", cores)
    far_g = lax.ppermute(near_g, "c", cores)
    near_half = lax.ppermute(half, "x", [(0, 1), (1, 0), (2, 3), (3, 2)])
    far_half = lax.ppermute(near_half, "c", cores)

    parts, weights, x_aligned, g_aligned = call(
        forward_kernel,
        [((8, 72, 384), BF16), ((384, 640), BF16), ((512, 640), BF16), ((512, 640), BF16)],
    )(received, residual, out_grad, far_x, far_g, gain)
    parts = lax.all_to_all(parts, MP, 0, 0)
    message, inverse = call(activation_kernel, [((8, 72, 384), BF16), ((8, 256), F32)])(parts)
    acts = lax.all_to_all(message, MP, 0, 0)
    terms, near_resid, far_resid = call(
        gradient_kernel,
        [((32, 64, 128), BF16), ((256, 640), F32), ((256, 640), BF16)],
        scalars=1,
    )(acts, weights, x_aligned, g_aligned, near_half, far_half, inverse, gain, signs, table, exponents)
    terms = lax.all_to_all(terms, ("z", "yl"), 0, 0)
    far_resid = lax.ppermute(far_resid, "c", cores)
    (resid_grad,) = call(resid_kernel, [((256, 576), BF16)])(out_grad, near_resid, far_resid)
    (share,) = call(total_kernel, [((32, 64, 128), BF16)])(terms)
    share = lax.all_to_all(share.reshape(256, 8, 128), ("z", "yl", "yh", "x"), 0, 0).reshape(32, 64, 128)
    other = lax.ppermute(share, "c", cores)
    (weight_grads,) = call(restore_kernel, [((3, 32, 4608), BF16)], scalars=1)(
        share, other, signs, table, exponents
    )
    return (resid_grad, weight_grads)


def solution(mesh):
    axes = ("z", "yl", "c", "yh", "x")
    fine = Mesh(mesh.devices.reshape(8, 4, 2, 2, 4), axes)
    rows = P(DP, MP)
    return jax.shard_map(
        per_device,
        mesh=fine,
        in_specs=(rows, rows, P(None, MP, None), P(), P(), P()),
        out_specs=(rows, P(None, MP, None)),
        check_vma=False,
    )
```

```python
import functools

import jax
import jax.numpy as jnp
import numpy as np
from jax import lax
from jax.experimental import pallas as pl
from jax.experimental.pallas import tpu as pltpu
from jax.sharding import Mesh
from jax.sharding import PartitionSpec as P

F32 = jnp.float32
BF16 = jnp.bfloat16
AXES = ("z", "yl", "c", "yh", "x")
DP = ("z", "yl", "c")
MP = ("yh", "x")
VMEM_LIMIT = 40 * 1024 * 1024
FEATURES = 4608
CONTRACT_LAST = (((1,), (1,)), ((), ()))
CONTRACT_FIRST = (((0,), (0,)), ((), ()))


def signed_hadamard():
    table = np.array([[1.0]], np.float32)
    for _ in range(7):
        table = np.block([[table, table], [table, -table]])
    return table


def gelu_parts(values):
    tanh_input = 0.7978845608 * (values + 0.044715 * values * values * values)
    tanhed = jnp.tanh(tanh_input)
    forward = 0.5 * values * (1.0 + tanhed)
    gelu_slope = 0.5 * (1.0 + tanhed) + 0.5 * values * (1.0 - tanhed * tanhed) * 0.7978845608 * (
        1.0 + 3.0 * 0.044715 * values * values
    )
    return (forward, gelu_slope)


def pieces(values):
    high = values.astype(BF16)
    rest = values - high.astype(F32)
    middle = rest.astype(BF16)
    low = (rest - middle.astype(F32)).astype(BF16)
    return (high, middle, low)


def dot(left, right, dims=(((1,), (0,)), ((), ()))):
    return lax.dot_general(left, right, dims, preferred_element_type=F32)


def places():
    odd = lax.axis_index("x") % 2
    pair = lax.axis_index("yh") * 2 + lax.axis_index("x") // 2
    return (lax.axis_index("c"), odd, pair * 9)


def local_rows(table_ref, first, odd):
    return [table_ref[pl.ds(first + 5 * odd + b, 1), :] for b in range(4)] + [table_ref[pl.ds(first + 4, 1), :]]


def own_rows(odd):
    return (
        pl.ds(pl.multiple_of(odd * 64, 64), 512),
        pl.ds(pl.multiple_of((1 - odd) * 512, 64), 64),
    )


def prepare_kernel(w_ref, send_ref, sems):
    core, _, _ = places()
    rows = pl.ds(pl.multiple_of(core * 16, 16), 16)
    copies = []
    for m in range(8):
        start = 9 * (m // 2)
        for b, block in enumerate([start + 5 * (m % 2) + b for b in range(4)] + [start + 4]):
            copies.append(
                pltpu.make_async_copy(
                    w_ref.at[:, rows, pl.ds(block * 128, 128)], send_ref.at[m, b], sems.at[m * 5 + b]
                )
            )
    for copy in copies:
        copy.start()
    for copy in copies:
        copy.wait()


def forward_kernel(recv_ref, x_ref, g_ref, far_x_ref, far_g_ref, gain_ref, part_ref, w_ref, xa_ref, ga_ref, half_ref):
    _, odd, first = places()
    for j in range(8):
        for b in range(5):
            for k in range(3):
                w_ref[k * 128 + j * 16 : k * 128 + j * 16 + 16, b * 128 : (b + 1) * 128] = recv_ref[j, b, k]
    main, half = own_rows(odd)
    mine = pl.ds(pl.multiple_of(512 + odd * 64, 64), 64)
    theirs = pl.ds(pl.multiple_of(576 - odd * 64, 64), 64)
    for part, (to_ref, refs) in enumerate(((xa_ref, (x_ref, far_x_ref)), (ga_ref, (g_ref, far_g_ref)))):
        for side, ref in enumerate(refs):
            tokens = pl.ds(side * 256, 256)
            to_ref[0:512, tokens] = ref[main, :]
            to_ref[mine, tokens] = ref[half, :]
            to_ref[theirs, tokens] = jnp.zeros((64, 256), BF16)
            half_ref[pl.ds(64 * part, 64), tokens] = ref[half, :]
    gained = w_ref[0:256].astype(F32) * jnp.concatenate(local_rows(gain_ref, first, odd), axis=1)
    high = gained.astype(BF16)
    low = (gained - high.astype(F32)).astype(BF16)
    gate_up = (dot(low, xa_ref[...]) + dot(high, xa_ref[...])).astype(BF16)
    down = dot(w_ref[256:384], ga_ref[...]).astype(BF16)
    wide = xa_ref[...].astype(F32)
    sums = jnp.sum(wide * wide, axis=0, keepdims=True)
    tail = stacked_pieces(sums)
    for j in range(8):
        x, yh = j % 4, j // 4
        part_ref[x, yh, 0:16, :] = gate_up[j * 16 : j * 16 + 16]
        part_ref[x, yh, 16:32, :] = gate_up[128 + j * 16 : 128 + j * 16 + 16]
        part_ref[x, yh, 32:48, :] = down[j * 16 : j * 16 + 16]
        part_ref[x, yh, 48:56, :] = tail


def stacked_pieces(row):
    place = lax.broadcasted_iota(jnp.int32, (8, 512), 0)
    tail = jnp.zeros((8, 512), F32)
    for i, piece in enumerate(pieces(row)):
        tail = jnp.where(place == i, piece.astype(F32), tail)
    return tail.astype(BF16)


def sum_kernel(parts_ref, out_ref):
    for yh in range(2):
        total = parts_ref[0, yh].astype(F32)
        for i in range(1, 4):
            total = total + parts_ref[i, yh].astype(F32)
        out_ref[yh, 0:48, :] = total[0:48].astype(BF16)
        out_ref[yh, 48:56, :] = stacked_pieces(total[48:49] + total[49:50] + total[50:51])


def activation_kernel(parts_ref, out_ref, inv_ref):
    for yh in range(2):
        total = parts_ref[0, yh].astype(F32) + parts_ref[1, yh].astype(F32)
        sums = total[48:49] + total[49:50] + total[50:51]
        inverse = lax.rsqrt(sums / FEATURES + 1e-06)
        inv_ref[...] = jnp.broadcast_to(inverse, (8, 512))
        gate_pre, up_proj, hidden_grad = total[0:16] * inverse, total[16:32] * inverse, total[32:48]
        activated, slope = gelu_parts(gate_pre)
        hidden = (activated * up_proj).astype(BF16)
        gate_grad = (hidden_grad * up_proj * slope).astype(BF16)
        up_grad = (hidden_grad * activated).astype(BF16)
        products = gate_grad.astype(F32) * gate_pre + up_grad.astype(F32) * up_proj
        tail = stacked_pieces(jnp.sum(products, axis=0, keepdims=True) / FEATURES)
        for i in range(4):
            out_ref[i, yh, 0:16, :] = gate_grad
            out_ref[i, yh, 16:32, :] = up_grad
            out_ref[i, yh, 32:48, :] = hidden
            out_ref[i, yh, 48:56, :] = tail


def gradient_kernel(
    acts_ref, w_ref, xa_ref, ga_ref, half_ref, inv_ref, gain_ref, sign_ref, table_ref, exps_ref,
    term_ref, near_ref, far_ref,
):
    _, odd, first = places()
    table = table_ref[...]
    sign = (2 * jnp.concatenate(local_rows(sign_ref, first, odd), axis=1) - 1).astype(F32)
    diagonal = lax.broadcasted_iota(jnp.int32, (128, 128), 0) == lax.broadcasted_iota(jnp.int32, (128, 128), 1)
    gain = jnp.concatenate(
        [
            jnp.sum(jnp.where(diagonal, row, 0.0), axis=1, keepdims=True)
            for row in local_rows(gain_ref, first, odd)
        ],
        axis=0,
    )
    acts = [
        jnp.concatenate([acts_ref[j % 4, j // 4, k * 16 : k * 16 + 16, :] for j in range(8)], axis=0)
        for k in range(3)
    ]
    tails = acts_ref[0, 0, 48:56, :].astype(F32)
    for j in range(1, 8):
        tails = tails + acts_ref[j % 4, j // 4, 48:56, :].astype(F32)
    row_mean = tails[0:1] + tails[1:2] + tails[2:3]
    inverse = inv_ref[0:1, :]
    theirs = (lax.broadcasted_iota(jnp.int32, (128, 512), 0) >= 64) == (odd == 0)
    shared = []
    for part, ref in enumerate((xa_ref, ga_ref)):
        other = half_ref[part * 64 : part * 64 + 64, :].astype(F32)
        shared.append(
            jnp.where(theirs, jnp.concatenate([other, other], axis=0), ref[512:640, :].astype(F32))
        )
    unit = jnp.concatenate([xa_ref[0:512, :].astype(F32), shared[0]], axis=0) * inverse
    normed = (unit * gain).astype(BF16)
    grads = jnp.concatenate([ga_ref[0:512, :], shared[1].astype(BF16)], axis=0)
    rights = (normed, normed, grads)
    for k in range(3):
        scale = jnp.left_shift(1, exps_ref[k]).astype(F32) * float(128.0**-0.5)
        terms = [
            dot(acts[k][:, s * 256 : s * 256 + 256], rights[k][:, s * 256 : s * 256 + 256], CONTRACT_LAST) * sign
            for s in range(2)
        ]
        for b in range(5):
            total = None
            for term in terms:
                high, middle, low = pieces(term[:, b * 128 : (b + 1) * 128])
                rotated = (dot(low, table) + dot(middle, table)) + dot(high, table)
                quantized = jnp.clip(rotated * scale, -127.0, 127.0).astype(BF16).astype(F32)
                total = quantized if total is None else total + quantized
            half = total.reshape(8, 2, 8, 128)
            if b < 4:
                term_ref[k * 8 + b] = half[:, 0].reshape(64, 128).astype(BF16)
                term_ref[k * 8 + 4 + b] = half[:, 1].reshape(64, 128).astype(BF16)
            else:
                chosen = jnp.where(odd == 1, half[:, 1], half[:, 0])
                term_ref[24 + k] = chosen.reshape(64, 128).astype(BF16)
    for s in range(27, 32):
        term_ref[s] = jnp.zeros((64, 128), BF16)
    normed_grad = dot(w_ref[0:256], jnp.concatenate(acts[0:2], axis=0), CONTRACT_FIRST)
    resid = inverse * (normed_grad * gain - unit * row_mean)
    main, half = own_rows(odd)
    shared_half = jnp.where(odd == 1, resid[576:640], resid[512:576])
    near_ref[main, :] = resid[0:512, 0:256]
    near_ref[half, :] = shared_half[:, 0:256]
    far_ref[main, :] = resid[0:512, 256:512].astype(BF16)
    far_ref[half, :] = shared_half[:, 256:512].astype(BF16)


def total_kernel(terms_ref, g_ref, near_ref, far_ref, share_ref, resid_ref):
    total = terms_ref[0].astype(F32)
    for i in range(1, 32):
        total = total + terms_ref[i].astype(F32)
    rounded = total.astype(BF16)
    for i in range(32):
        share_ref[i] = rounded
    resid_ref[...] = (g_ref[...].astype(F32) + (near_ref[...] + far_ref[...].astype(F32))).astype(BF16)


def restore_kernel(near_ref, far_ref, sign_ref, table_ref, exps_ref, out_ref):
    table = table_ref[...]
    core, _, _ = places()
    for k in range(3):
        e = exps_ref[k]
        factor = jnp.where(e == 3, 2.0**-9, jnp.where(e == 4, 2.0**-10, jnp.where(e == 5, 2.0**-11, 2.0**-12)))
        factor = factor.astype(F32) * float(128.0**-0.5)
        for q, share_ref in ((core, near_ref), (1 - core, far_ref)):
            rows = pl.ds(pl.multiple_of(16 * q, 16), 16)

            def put(block, low_half, high_half):
                sign = (2 * sign_ref[block : block + 1, :] - 1).astype(F32) * factor
                both = jnp.concatenate([low_half, high_half], axis=0) * sign
                out_ref[k, rows, block * 128 : (block + 1) * 128] = both.astype(BF16)

            for b in range(4):
                halves = [dot(share_ref[k * 8 + 4 * i + b], table) for i in range(2)]
                for m in range(8):
                    put(
                        9 * (m // 2) + 5 * (m % 2) + b,
                        halves[0][m * 8 : m * 8 + 8],
                        halves[1][m * 8 : m * 8 + 8],
                    )
            shared = dot(share_ref[24 + k], table)
            for p in range(4):
                put(9 * p + 4, shared[16 * p : 16 * p + 8], shared[16 * p + 8 : 16 * p + 16])


def call(kernel, outs, scalars=0, scratch=(), space=pltpu.VMEM):
    def run(*operands):
        count = len(operands)
        spaces = [pltpu.SMEM if i >= count - scalars else space for i in range(count)]
        return pl.pallas_call(
            kernel,
            out_shape=[jax.ShapeDtypeStruct(shape, dtype) for shape, dtype in outs],
            in_specs=[pl.BlockSpec(memory_space=place) for place in spaces],
            out_specs=[pl.BlockSpec(memory_space=space) for _ in outs],
            scratch_shapes=list(scratch),
            compiler_params=pltpu.CompilerParams(vmem_limit_bytes=VMEM_LIMIT),
            name=kernel.__name__,
        )(*operands)

    return run


def per_device(residual, out_grad, ffn_weights, norm_gain, exponents, sign_bits):
    gain = norm_gain.reshape(36, 128)
    signs = sign_bits.reshape(36, 128)
    table = jnp.asarray(signed_hadamard(), BF16)
    cores = [(0, 1), (1, 0)]
    x_cols, g_cols = residual.T, out_grad.T

    (send,) = call(
        prepare_kernel, [((8, 5, 3, 16, 128), BF16)], scratch=[pltpu.SemaphoreType.DMA((40,))], space=pl.ANY
    )(ffn_weights)
    received = lax.all_to_all(send.reshape(8, 240, 128), AXES, 0, 0, axis_index_groups=near_groups())
    near_x, near_g, _ = lax.optimization_barrier((x_cols, g_cols, send))
    far_x = lax.ppermute(near_x, "c", cores)
    far_g = lax.ppermute(near_g, "c", cores)
    parts, weights, x_aligned, g_aligned, half = call(
        forward_kernel,
        [((4, 2, 56, 512), BF16), ((384, 640), BF16), ((640, 512), BF16), ((640, 512), BF16), ((128, 512), BF16)],
    )(received.reshape(8, 5, 3, 16, 128), x_cols, g_cols, far_x, far_g, gain)

    other_half = lax.ppermute(half, "x", [(0, 1), (1, 0), (2, 3), (3, 2)])
    parts = lax.all_to_all(parts.reshape(4, 112, 512), "x", 0, 0)
    parts, other_half = lax.optimization_barrier((parts, other_half))
    (sums,) = call(sum_kernel, [((2, 56, 512), BF16)])(parts.reshape(4, 2, 56, 512))
    sums = lax.all_gather(sums, "yh", axis=0)
    message, inverse = call(activation_kernel, [((4, 2, 56, 512), BF16), ((8, 512), F32)])(sums)
    acts = lax.all_to_all(message.reshape(4, 112, 512), "x", 0, 0).reshape(4, 2, 56, 512)
    terms, near_resid, far_resid = call(
        gradient_kernel,
        [((32, 64, 128), BF16), ((576, 256), F32), ((576, 256), BF16)],
        scalars=1,
    )(acts, weights, x_aligned, g_aligned, other_half, inverse, gain, signs, table, exponents)
    terms = lax.all_to_all(terms, ("z", "yl"), 0, 0)
    far_resid = lax.ppermute(far_resid, "c", cores)
    share, resid_cols = call(total_kernel, [((32, 64, 128), BF16), ((576, 256), BF16)])(
        terms, g_cols, near_resid, far_resid
    )
    share = lax.all_to_all(share.reshape(256, 8, 128), ("z", "yl", "yh", "x"), 0, 0).reshape(32, 64, 128)
    other = lax.ppermute(share, "c", cores)
    (weight_grads,) = call(restore_kernel, [((3, 32, 4608), BF16)], scalars=1)(
        share, other, signs, table, exponents
    )
    return (resid_cols.T, weight_grads)


def near_groups():
    def flat(z, yl, c, yh, x):
        return (((z * 4 + yl) * 2 + c) * 2 + yh) * 4 + x

    return [
        [flat(z, 3 - yl if yh else yl, c, yh, x) for yh in range(2) for x in range(4)]
        for z in range(8)
        for yl in range(4)
        for c in range(2)
    ]


def solution(mesh):
    fine = Mesh(mesh.devices.reshape(8, 4, 2, 2, 4), AXES)
    rows = P(DP, MP)
    return jax.shard_map(
        per_device,
        mesh=fine,
        in_specs=(rows, rows, P(None, MP, None), P(), P(), P()),
        out_specs=(rows, P(None, MP, None)),
        check_vma=False,
    )
```

```python
import functools

import jax
import jax.numpy as jnp
import numpy as np
from jax import lax
from jax.experimental import pallas as pl
from jax.experimental.pallas import tpu as pltpu
from jax.sharding import Mesh
from jax.sharding import PartitionSpec as P

F32 = jnp.float32
BF16 = jnp.bfloat16
AXES = ("z", "yl", "c", "yh", "x")
DP = ("z", "yl", "c")
MP = ("yh", "x")
VMEM_LIMIT = 20 * 1024 * 1024
FEATURES = 4608
CONTRACT_LAST = (((1,), (1,)), ((), ()))
CONTRACT_FIRST = (((0,), (0,)), ((), ()))


def signed_hadamard():
    table = np.array([[1.0]], np.float32)
    for _ in range(7):
        table = np.block([[table, table], [table, -table]])
    return table


def gelu_parts(values):
    tanh_input = 0.7978845608 * (values + 0.044715 * values * values * values)
    tanhed = jnp.tanh(tanh_input)
    forward = 0.5 * values * (1.0 + tanhed)
    gelu_slope = 0.5 * (1.0 + tanhed) + 0.5 * values * (1.0 - tanhed * tanhed) * 0.7978845608 * (
        1.0 + 3.0 * 0.044715 * values * values
    )
    return (forward, gelu_slope)


def pieces(values):
    high = values.astype(BF16)
    rest = values - high.astype(F32)
    middle = rest.astype(BF16)
    low = (rest - middle.astype(F32)).astype(BF16)
    return (high, middle, low)


def dot(left, right, dims=(((1,), (0,)), ((), ()))):
    return lax.dot_general(left, right, dims, preferred_element_type=F32)


def places():
    odd = lax.axis_index("x") % 2
    pair = lax.axis_index("yh") * 2 + lax.axis_index("x") // 2
    return (lax.axis_index("c"), odd, pair * 9)


def local_rows(table_ref, first, odd):
    return [table_ref[pl.ds(first + 5 * odd + b, 1), :] for b in range(4)] + [table_ref[pl.ds(first + 4, 1), :]]


def own_rows(odd):
    return (
        pl.ds(pl.multiple_of(odd * 64, 64), 512),
        pl.ds(pl.multiple_of((1 - odd) * 512, 64), 64),
    )


def prepare_kernel(w_ref, send_ref):
    core, _, _ = places()
    rows = pl.ds(pl.multiple_of(core * 16, 16), 16)
    for m in range(8):
        start = 9 * (m // 2)
        for b, block in enumerate([start + 5 * (m % 2) + b for b in range(4)] + [start + 4]):
            for k in range(3):
                send_ref[m, b, k] = w_ref[k, rows, block * 128 : (block + 1) * 128]


def align_kernel(x_ref, g_ref, far_x_ref, far_g_ref, exps_ref, xa_ref, ga_ref, half_ref, tail_ref, scale_ref):
    place = lax.broadcasted_iota(jnp.int32, (8, 128), 0)
    scales = jnp.zeros((8, 128), F32)
    for k in range(3):
        e = exps_ref[k]
        up = jnp.where(e == 3, 8.0, jnp.where(e == 4, 16.0, jnp.where(e == 5, 32.0, 64.0)))
        down = jnp.where(e == 3, 2.0**-9, jnp.where(e == 4, 2.0**-10, jnp.where(e == 5, 2.0**-11, 2.0**-12)))
        scales = jnp.where(place == k, up, jnp.where(place == 3 + k, down, scales))
    scale_ref[...] = scales * float(128.0**-0.5)
    _, odd, _ = places()
    main, half = own_rows(odd)
    mine = pl.ds(pl.multiple_of(512 + odd * 64, 64), 64)
    theirs = pl.ds(pl.multiple_of(576 - odd * 64, 64), 64)
    for part, (to_ref, refs) in enumerate(((xa_ref, (x_ref, far_x_ref)), (ga_ref, (g_ref, far_g_ref)))):
        for side, ref in enumerate(refs):
            tokens = pl.ds(side * 256, 256)
            to_ref[0:512, tokens] = ref[main, :]
            to_ref[mine, tokens] = ref[half, :]
            to_ref[theirs, tokens] = jnp.zeros((64, 256), BF16)
            half_ref[pl.ds(64 * part, 64), tokens] = ref[half, :]
    wide = xa_ref[...].astype(F32)
    tail_ref[...] = stacked_pieces(jnp.sum(wide * wide, axis=0, keepdims=True))


def forward_kernel(recv_ref, xa_ref, ga_ref, tail_ref, gain_ref, part_ref, w_ref):
    _, odd, first = places()
    for j in range(8):
        for b in range(5):
            for k in range(3):
                w_ref[k * 128 + j * 16 : k * 128 + j * 16 + 16, b * 128 : (b + 1) * 128] = recv_ref[j, b, k]
    gained = w_ref[0:256].astype(F32) * jnp.concatenate(local_rows(gain_ref, first, odd), axis=1)
    high = gained.astype(BF16)
    low = (gained - high.astype(F32)).astype(BF16)
    gate_up = (dot(low, xa_ref[...]) + dot(high, xa_ref[...])).astype(BF16)
    down = dot(w_ref[256:384], ga_ref[...]).astype(BF16)
    tail = tail_ref[...]
    for j in range(8):
        x, yh = j % 4, j // 4
        part_ref[x, yh, 0:16, :] = gate_up[j * 16 : j * 16 + 16]
        part_ref[x, yh, 16:32, :] = gate_up[128 + j * 16 : 128 + j * 16 + 16]
        part_ref[x, yh, 32:48, :] = down[j * 16 : j * 16 + 16]
        part_ref[x, yh, 48:56, :] = tail


def stacked_pieces(row):
    place = lax.broadcasted_iota(jnp.int32, (8, 512), 0)
    tail = jnp.zeros((8, 512), F32)
    for i, piece in enumerate(pieces(row)):
        tail = jnp.where(place == i, piece.astype(F32), tail)
    return tail.astype(BF16)


def sum_kernel(parts_ref, _, out_ref, own_ref):
    for yh in range(2):
        total = parts_ref[0, yh].astype(F32)
        for i in range(1, 4):
            total = total + parts_ref[i, yh].astype(F32)
        own_ref[yh] = total[0:48]
        out_ref[yh, 0:48, :] = total[0:48].astype(BF16)
        out_ref[yh, 48:56, :] = stacked_pieces(total[48:49] + total[49:50] + total[50:51])


def activation_kernel(parts_ref, own_ref, out_ref, inv_ref):
    high = lax.axis_index("yh") == 1
    for yh in range(2):
        others = [parts_ref[i, yh, 0:48, :].astype(F32) for i in range(2)]
        total = own_ref[yh] + jnp.where(high, others[0], others[1])
        tails = parts_ref[0, yh, 48:56, :].astype(F32) + parts_ref[1, yh, 48:56, :].astype(F32)
        sums = tails[0:1] + tails[1:2] + tails[2:3]
        inverse = lax.rsqrt(sums / FEATURES + 1e-06)
        inv_ref[...] = jnp.broadcast_to(inverse, (8, 512))
        gate_pre, up_proj, hidden_grad = total[0:16] * inverse, total[16:32] * inverse, total[32:48]
        activated, slope = gelu_parts(gate_pre)
        hidden = (activated * up_proj).astype(BF16)
        gate_grad = (hidden_grad * up_proj * slope).astype(BF16)
        up_grad = (hidden_grad * activated).astype(BF16)
        products = gate_grad.astype(F32) * gate_pre + up_grad.astype(F32) * up_proj
        tail = stacked_pieces(jnp.sum(products, axis=0, keepdims=True) / FEATURES)
        for i in range(4):
            out_ref[i, yh, 0:16, :] = gate_grad
            out_ref[i, yh, 16:32, :] = up_grad
            out_ref[i, yh, 32:48, :] = hidden
            out_ref[i, yh, 48:56, :] = tail


def feature_column(table_ref, first, odd):
    diagonal = lax.broadcasted_iota(jnp.int32, (128, 128), 0) == lax.broadcasted_iota(jnp.int32, (128, 128), 1)
    rows = local_rows(table_ref, first, odd)
    return jnp.concatenate(
        [jnp.sum(jnp.where(diagonal, row.astype(F32), 0.0), axis=1, keepdims=True) for row in rows], axis=0
    )


def gathered_acts(acts_ref, k):
    return jnp.concatenate([acts_ref[j % 4, j // 4, k * 16 : k * 16 + 16, :] for j in range(8)], axis=0)


def gradient_kernel(
    acts_ref, xa_ref, ga_ref, half_ref, inv_ref, gain_ref, sign_ref, table_ref, scale_ref, term_ref
):
    _, odd, first_block = places()
    table = table_ref[...]
    sign = 2.0 * feature_column(sign_ref, first_block, odd) - 1.0
    gain = feature_column(gain_ref, first_block, odd) * sign
    theirs = (lax.broadcasted_iota(jnp.int32, (128, 512), 0) >= 64) == (odd == 0)
    rights = []
    for part, (ref, factor) in enumerate(((xa_ref, inv_ref[0:1, :]), (ga_ref, None))):
        other = half_ref[part * 64 : part * 64 + 64, :].astype(F32)
        shared = jnp.where(theirs, jnp.concatenate([other, other], axis=0), ref[512:640, :].astype(F32))
        values = jnp.concatenate([ref[0:512, :].astype(F32), shared], axis=0)
        rights.append((values * sign if factor is None else values * factor * gain).astype(BF16))
    rights = (rights[0], rights[0], rights[1])
    for k in range(3):
        acts = gathered_acts(acts_ref, k)
        scale = scale_ref[k : k + 1, 0:1]
        terms = jnp.concatenate(
            [
                dot(acts[:, s * 256 : s * 256 + 256], rights[k][:, s * 256 : s * 256 + 256], CONTRACT_LAST)
                for s in range(2)
            ],
            axis=0,
        )
        for first in (0, 256, 512):
            width = min(256, 640 - first)
            block = terms[:, first : first + width]
            high = block.astype(BF16)
            low = (block - high.astype(F32)).astype(BF16)
            part = table[0:width, 0:width]
            rotated = dot(low, part) + dot(high, part)
            quantized = jnp.clip(rotated * scale, -127.0, 127.0).astype(BF16).astype(F32)
            total = quantized[0:128] + quantized[128:256]
            for b in range(first // 128, (first + width) // 128):
                half = total[:, b * 128 - first : b * 128 - first + 128].reshape(8, 2, 8, 128)
                if b < 4:
                    term_ref[k * 8 + b] = half[:, 0].reshape(64, 128).astype(BF16)
                    term_ref[k * 8 + 4 + b] = half[:, 1].reshape(64, 128).astype(BF16)
                else:
                    chosen = jnp.where(odd == 1, half[:, 1], half[:, 0])
                    term_ref[24 + k] = chosen.reshape(64, 128).astype(BF16)
    for s in range(27, 32):
        term_ref[s] = jnp.zeros((64, 128), BF16)


def resid_kernel(acts_ref, w_ref, xa_ref, inv_ref, gain_ref, _, near_ref, far_ref):
    _, odd, first = places()
    gain = feature_column(gain_ref, first, odd)
    inverse = inv_ref[0:1, :]
    tails = acts_ref[0, 0, 48:56, :].astype(F32)
    for j in range(1, 8):
        tails = tails + acts_ref[j % 4, j // 4, 48:56, :].astype(F32)
    row_mean = tails[0:1] + tails[1:2] + tails[2:3]
    pair = jnp.concatenate([gathered_acts(acts_ref, k) for k in range(2)], axis=0)
    normed_grad = dot(w_ref[0:256], pair, CONTRACT_FIRST)
    unit = xa_ref[...].astype(F32) * inverse
    resid = inverse * (normed_grad * gain - unit * row_mean)
    main, half = own_rows(odd)
    shared_half = jnp.where(odd == 1, resid[576:640], resid[512:576])
    near_ref[main, :] = resid[0:512, 0:256]
    near_ref[half, :] = shared_half[:, 0:256]
    far_ref[main, :] = resid[0:512, 256:512].astype(BF16)
    far_ref[half, :] = shared_half[:, 256:512].astype(BF16)


def finish_kernel(g_ref, near_ref, far_ref, out_ref, done_ref):
    out_ref[...] = (g_ref[...].astype(F32) + (near_ref[...] + far_ref[...].astype(F32))).astype(BF16)
    done_ref[...] = jnp.zeros((8, 128), F32)


def total_kernel(terms_ref, _, share_ref):
    totals = []
    for yh in range(2):
        total = terms_ref[yh].astype(F32)
        for i in range(1, 32):
            total = total + terms_ref[2 * i + yh].astype(F32)
        totals.append(total)
    for x in range(4):
        both = jnp.concatenate([total[x * 8 : x * 8 + 8] for total in totals], axis=0).astype(BF16)
        for i in range(32):
            share_ref[i * 4 + x] = both


def received_rows(m):
    start = 8 * (2 * (m % 4) + m // 4)
    return slice(start, start + 8)


def restore_half(q, share_ref, sign_ref, table_ref, scale_ref, out_ref, held, sems):
    table = table_ref[0:128, 0:128]
    copies = []
    for k in range(3):
        factor = scale_ref[3 + k : 4 + k, :]

        def put(block, low_half, high_half):
            sign = (2 * sign_ref[block : block + 1, :] - 1).astype(F32) * factor
            both = jnp.concatenate([low_half, high_half], axis=0) * sign
            held[k, :, block * 128 : (block + 1) * 128] = both.astype(BF16)

        for b in range(4):
            halves = [dot(share_ref[k * 8 + 4 * i + b], table) for i in range(2)]
            for m in range(8):
                rows = received_rows(m)
                put(9 * (m // 2) + 5 * (m % 2) + b, halves[0][rows], halves[1][rows])
        shared = dot(share_ref[24 + k], table)
        for p in range(4):
            put(9 * p + 4, shared[received_rows(2 * p)], shared[received_rows(2 * p + 1)])
        rows = pl.ds(pl.multiple_of(16 * q, 16), 16)
        copy = pltpu.make_async_copy(held.at[k], out_ref.at[k, rows, :], sems.at[k])
        copy.start()
        copies.append(copy)
    for copy in copies:
        copy.wait()


def near_restore_kernel(share_ref, sign_ref, table_ref, scale_ref, out_ref, held, sems):
    restore_half(lax.axis_index("c"), share_ref, sign_ref, table_ref, scale_ref, out_ref, held, sems)


def far_restore_kernel(share_ref, sign_ref, table_ref, scale_ref, _, out_ref, held, sems):
    restore_half(1 - lax.axis_index("c"), share_ref, sign_ref, table_ref, scale_ref, out_ref, held, sems)


def call(kernel, outs, scalars=0, scratch=(), anywhere=(), out_space=pltpu.VMEM, aliases=None, limit=VMEM_LIMIT):
    def run(*operands):
        count = len(operands)
        spaces = [
            pltpu.SMEM if i >= count - scalars else pl.ANY if i in anywhere else pltpu.VMEM for i in range(count)
        ]
        return pl.pallas_call(
            kernel,
            out_shape=[jax.ShapeDtypeStruct(shape, dtype) for shape, dtype in outs],
            in_specs=[pl.BlockSpec(memory_space=place) for place in spaces],
            out_specs=[pl.BlockSpec(memory_space=out_space) for _ in outs],
            scratch_shapes=list(scratch),
            input_output_aliases=aliases or {},
            compiler_params=pltpu.CompilerParams(vmem_limit_bytes=limit),
            cost_estimate=pl.CostEstimate(flops=10**9, bytes_accessed=10**6, transcendentals=0),
            name=kernel.__name__,
        )(*operands)

    return run


def per_device(residual, out_grad, ffn_weights, norm_gain, exponents, sign_bits):
    gain = norm_gain.reshape(36, 128)
    signs = sign_bits.reshape(36, 128)
    table = jnp.asarray(np.kron(np.eye(2), signed_hadamard()), BF16)
    cores = [(0, 1), (1, 0)]
    x_cols, g_cols = residual.T, out_grad.T
    rows = ((640, 512), BF16)

    (send,) = call(prepare_kernel, [((8, 5, 3, 16, 128), BF16)])(ffn_weights)
    received = lax.all_to_all(send.reshape(8, 240, 128), AXES, 0, 0, axis_index_groups=near_groups())
    near_x, near_g, _ = lax.optimization_barrier((x_cols, g_cols, send))
    far_x = lax.ppermute(near_x, "c", cores)
    far_g = lax.ppermute(near_g, "c", cores)
    xa, ga, half, tail, scales = call(
        align_kernel, [rows, rows, ((128, 512), BF16), ((8, 512), BF16), ((8, 128), F32)], scalars=1
    )(x_cols, g_cols, far_x, far_g, exponents)
    parts, weights = call(forward_kernel, [((4, 2, 56, 512), BF16), ((384, 640), BF16)])(
        received.reshape(8, 5, 3, 16, 128), xa, ga, tail, gain
    )

    other_half = lax.ppermute(half, "x", [(0, 1), (1, 0), (2, 3), (3, 2)])
    parts = lax.all_to_all(parts.reshape(4, 112, 512), "x", 0, 0).reshape(4, 2, 56, 512)
    sums, own = call(sum_kernel, [((2, 56, 512), BF16), ((2, 48, 512), F32)], anywhere=(1,))(parts, other_half)
    sums = lax.all_gather(sums, "yh", axis=0)
    message, inverse = call(activation_kernel, [((4, 2, 56, 512), BF16), ((8, 512), F32)])(sums, own)
    acts = lax.all_to_all(message.reshape(4, 112, 512), "x", 0, 0).reshape(4, 2, 56, 512)
    (terms,) = call(gradient_kernel, [((32, 64, 128), BF16)])(
        acts, xa, ga, other_half, inverse, gain, signs, table, scales
    )

    summands = lax.all_to_all(terms.reshape(64, 32, 128), ("z", "yl", "yh"), 0, 0)
    near_resid, far_resid = call(resid_kernel, [((576, 256), F32), ((576, 256), BF16)], anywhere=(5,))(
        acts, weights, xa, inverse, gain, terms
    )
    far_resid = lax.ppermute(far_resid, "c", cores)
    resid_cols, done = call(finish_kernel, [((576, 256), BF16), ((8, 128), F32)])(g_cols, near_resid, far_resid)
    (share,) = call(total_kernel, [((128, 16, 128), BF16)])(summands, done)
    share = lax.all_to_all(share, ("z", "yl", "x"), 0, 0).reshape(32, 64, 128)
    other = lax.ppermute(share, "c", cores)
    scratch = [pltpu.VMEM((3, 16, 4608), BF16), pltpu.SemaphoreType.DMA((3,))]
    out = [((3, 32, 4608), BF16)]
    (half_done,) = call(near_restore_kernel, out, scratch=scratch, out_space=pl.ANY)(share, signs, table, scales)
    (weight_grads,) = call(
        far_restore_kernel, out, scratch=scratch, anywhere=(4,), out_space=pl.ANY, aliases={4: 0}
    )(other, signs, table, scales, half_done)
    return (resid_cols.T, weight_grads)


def near_groups():
    def flat(z, yl, c, yh, x):
        return (((z * 4 + yl) * 2 + c) * 2 + yh) * 4 + x

    return [
        [flat(z, 3 - yl if yh else yl, c, yh, x) for yh in range(2) for x in range(4)]
        for z in range(8)
        for yl in range(4)
        for c in range(2)
    ]


def solution(mesh):
    fine = Mesh(mesh.devices.reshape(8, 4, 2, 2, 4), AXES)
    rows = P(DP, MP)
    return jax.shard_map(
        per_device,
        mesh=fine,
        in_specs=(rows, rows, P(None, MP, None), P(), P(), P()),
        out_specs=(rows, P(None, MP, None)),
        check_vma=False,
    )
```

```python
import functools

import jax
import jax.numpy as jnp
import numpy as np
from jax import lax
from jax.experimental import pallas as pl
from jax.experimental.pallas import tpu as pltpu
from jax.sharding import Mesh
from jax.sharding import PartitionSpec as P

F32 = jnp.float32
BF16 = jnp.bfloat16
AXES = ("z", "yl", "c", "yh", "x")
DP = ("z", "yl", "c")
MP = ("yh", "x")
VMEM_LIMIT = 20 * 1024 * 1024
FEATURES = 4608
CONTRACT_LAST = (((1,), (1,)), ((), ()))
CONTRACT_FIRST = (((0,), (0,)), ((), ()))


def signed_hadamard():
    table = np.array([[1.0]], np.float32)
    for _ in range(7):
        table = np.block([[table, table], [table, -table]])
    return table


def gelu_parts(values):
    tanh_input = 0.7978845608 * (values + 0.044715 * values * values * values)
    tanhed = jnp.tanh(tanh_input)
    forward = 0.5 * values * (1.0 + tanhed)
    gelu_slope = 0.5 * (1.0 + tanhed) + 0.5 * values * (1.0 - tanhed * tanhed) * 0.7978845608 * (
        1.0 + 3.0 * 0.044715 * values * values
    )
    return (forward, gelu_slope)


def pieces(values):
    high = values.astype(BF16)
    rest = values - high.astype(F32)
    middle = rest.astype(BF16)
    low = (rest - middle.astype(F32)).astype(BF16)
    return (high, middle, low)


def dot(left, right, dims=(((1,), (0,)), ((), ()))):
    return lax.dot_general(left, right, dims, preferred_element_type=F32)


def places():
    odd = lax.axis_index("x") % 2
    pair = lax.axis_index("yh") * 2 + lax.axis_index("x") // 2
    return (lax.axis_index("c"), odd, pair * 9)


def local_rows(table_ref, first, odd):
    return [table_ref[pl.ds(first + 5 * odd + b, 1), :] for b in range(4)] + [table_ref[pl.ds(first + 4, 1), :]]


def own_rows(odd):
    return (
        pl.ds(pl.multiple_of(odd * 64, 64), 512),
        pl.ds(pl.multiple_of((1 - odd) * 512, 64), 64),
    )


def prepare_kernel(w_ref, send_ref, held, packed, in_sems, out_sems):
    core, _, _ = places()
    rows = pl.ds(pl.multiple_of(core * 16, 16), 16)
    loads = [
        pltpu.make_async_copy(w_ref.at[:, rows, pl.ds(p * 1152, 1152)], held.at[p], in_sems.at[p]) for p in range(4)
    ]
    for load in loads:
        load.start()
    lane = lax.broadcasted_iota(jnp.int32, (16, 128), 1)
    stores = []
    for m in range(8):
        pair, odd = m // 2, m % 2
        if odd == 0:
            loads[pair].wait()
        for b in range(4):
            column = (5 * odd + b) * 128
            for k in range(3):
                packed[m, b * 3 + k] = held[pair, k, :, column : column + 128]
        gate, up, down = [held[pair, k, :, 512:640] for k in range(3)]
        turned = pltpu.roll(up.astype(F32), 64, 1)
        packed[m, 12] = jnp.where((lane >= 64) == (odd == 1), gate.astype(F32), turned).astype(BF16)
        packed[m, 13] = down
        store = pltpu.make_async_copy(packed.at[m], send_ref.at[m], out_sems.at[m])
        store.start()
        stores.append(store)
    for store in stores:
        store.wait()


def join_kernel(x_ref, g_ref, out_ref):
    out_ref[0:576, :] = x_ref[...]
    out_ref[576:1152, :] = g_ref[...]


def align_kernel(near_ref, far_ref, exps_ref, xa_ref, ga_ref, half_ref, tail_ref, scale_ref):
    place = lax.broadcasted_iota(jnp.int32, (8, 128), 0)
    scales = jnp.zeros((8, 128), F32)
    for k in range(3):
        e = exps_ref[k]
        up = jnp.where(e == 3, 8.0, jnp.where(e == 4, 16.0, jnp.where(e == 5, 32.0, 64.0)))
        down = jnp.where(e == 3, 2.0**-9, jnp.where(e == 4, 2.0**-10, jnp.where(e == 5, 2.0**-11, 2.0**-12)))
        scales = jnp.where(place == k, up, jnp.where(place == 3 + k, down, scales))
    scale_ref[...] = scales * float(128.0**-0.5)
    _, odd, _ = places()
    main, half = pl.multiple_of(odd * 64, 64), pl.multiple_of((1 - odd) * 512, 64)
    mine = pl.ds(pl.multiple_of(512 + odd * 64, 64), 64)
    theirs = pl.ds(pl.multiple_of(576 - odd * 64, 64), 64)
    for part, to_ref in enumerate((xa_ref, ga_ref)):
        for side, ref in enumerate((near_ref, far_ref)):
            tokens = pl.ds(side * 256, 256)
            rows = ref[pl.ds(576 * part + half, 64), :]
            to_ref[0:512, tokens] = ref[pl.ds(576 * part + main, 512), :]
            to_ref[mine, tokens] = rows
            to_ref[theirs, tokens] = jnp.zeros((64, 256), BF16)
            half_ref[pl.ds(64 * part, 64), tokens] = rows
    wide = xa_ref[...].astype(F32)
    tail_ref[...] = stacked_pieces(jnp.sum(wide * wide, axis=0, keepdims=True))


def forward_kernel(recv_ref, xa_ref, ga_ref, tail_ref, gain_ref, _, part_ref, w_ref):
    _, odd, first = places()
    for j in range(8):
        for k in range(3):
            rows = slice(k * 128 + j * 16, k * 128 + j * 16 + 16)
            for b in range(4):
                w_ref[rows, b * 128 : (b + 1) * 128] = recv_ref[j, b * 3 + k]
        w_ref[j * 16 : j * 16 + 16, 512:640] = recv_ref[j, 12]
        w_ref[128 + j * 16 : 128 + j * 16 + 16, 512:640] = pltpu.roll(recv_ref[j, 12].astype(F32), 64, 1).astype(BF16)
        w_ref[256 + j * 16 : 256 + j * 16 + 16, 512:640] = recv_ref[j, 13]
    gained = w_ref[0:256].astype(F32) * jnp.concatenate(local_rows(gain_ref, first, odd), axis=1)
    high = gained.astype(BF16)
    low = (gained - high.astype(F32)).astype(BF16)
    gate_up = (dot(low, xa_ref[...]) + dot(high, xa_ref[...])).astype(BF16)
    down = dot(w_ref[256:384], ga_ref[...]).astype(BF16)
    tail = tail_ref[...]
    for x in range(4):
        for yh in range(2):
            j = 4 * yh + x
            for k, source in enumerate((gate_up[0:128], gate_up[128:256], down)):
                start = yh * 48 + k * 16
                part_ref[x, start : start + 16, :] = source[j * 16 : j * 16 + 16]
        part_ref[x, 96:104, :] = tail


def stacked_pieces(row):
    place = lax.broadcasted_iota(jnp.int32, (8, 512), 0)
    tail = jnp.zeros((8, 512), F32)
    for i, piece in enumerate(pieces(row)):
        tail = jnp.where(place == i, piece.astype(F32), tail)
    return tail.astype(BF16)


def sum_kernel(parts_ref, out_ref, own_ref):
    total = parts_ref[0].astype(F32)
    for i in range(1, 4):
        total = total + parts_ref[i].astype(F32)
    own_ref[...] = total[0:96]
    out_ref[0:96, :] = total[0:96].astype(BF16)
    out_ref[96:104, :] = stacked_pieces(total[96:97] + total[97:98] + total[98:99])


def activation_kernel(parts_ref, own_ref, out_ref, inv_ref):
    high = lax.axis_index("yh") == 1
    tails = parts_ref[0, 96:104, :].astype(F32) + parts_ref[1, 96:104, :].astype(F32)
    sums = tails[0:1] + tails[1:2] + tails[2:3]
    inverse = lax.rsqrt(sums / FEATURES + 1e-06)
    inv_ref[...] = jnp.broadcast_to(inverse, (8, 512))
    others = [parts_ref[i, 0:96, :].astype(F32) for i in range(2)]
    total = own_ref[...] + jnp.where(high, others[0], others[1])
    mean = jnp.zeros((1, 512), F32)
    for yh in range(2):
        start = yh * 48
        gate_pre = total[start : start + 16] * inverse
        up_proj = total[start + 16 : start + 32] * inverse
        hidden_grad = total[start + 32 : start + 48]
        activated, slope = gelu_parts(gate_pre)
        hidden = (activated * up_proj).astype(BF16)
        gate_grad = (hidden_grad * up_proj * slope).astype(BF16)
        up_grad = (hidden_grad * activated).astype(BF16)
        products = gate_grad.astype(F32) * gate_pre + up_grad.astype(F32) * up_proj
        mean = mean + jnp.sum(products, axis=0, keepdims=True) / FEATURES
        for i in range(4):
            out_ref[i, start : start + 16, :] = gate_grad
            out_ref[i, start + 16 : start + 32, :] = up_grad
            out_ref[i, start + 32 : start + 48, :] = hidden
    tail = stacked_pieces(mean)
    for i in range(4):
        out_ref[i, 96:104, :] = tail


def feature_column(table_ref, first, odd):
    diagonal = lax.broadcasted_iota(jnp.int32, (128, 128), 0) == lax.broadcasted_iota(jnp.int32, (128, 128), 1)
    rows = local_rows(table_ref, first, odd)
    return jnp.concatenate(
        [jnp.sum(jnp.where(diagonal, row.astype(F32), 0.0), axis=1, keepdims=True) for row in rows], axis=0
    )


def gathered_acts(acts_ref, k):
    starts = [(j % 4, j // 4 * 48 + k * 16) for j in range(8)]
    return jnp.concatenate([acts_ref[x, start : start + 16, :] for x, start in starts], axis=0)


def gradient_kernel(
    acts_ref, xa_ref, ga_ref, half_ref, inv_ref, gain_ref, sign_ref, table_ref, scale_ref, out_ref, term_ref, sems
):
    _, odd, first_block = places()
    table = table_ref[...]
    sign = 2.0 * feature_column(sign_ref, first_block, odd) - 1.0
    gain = feature_column(gain_ref, first_block, odd) * sign
    theirs = (lax.broadcasted_iota(jnp.int32, (128, 512), 0) >= 64) == (odd == 0)
    rights = []
    for part, (ref, factor) in enumerate(((xa_ref, inv_ref[0:1, :]), (ga_ref, None))):
        other = half_ref[part * 64 : part * 64 + 64, :].astype(F32)
        shared = jnp.where(theirs, jnp.concatenate([other, other], axis=0), ref[512:640, :].astype(F32))
        values = jnp.concatenate([ref[0:512, :].astype(F32), shared], axis=0)
        rights.append((values * sign if factor is None else values * factor * gain).astype(BF16))
    rights = (rights[0], rights[0], rights[1])
    for s in range(27, 32):
        term_ref[s] = jnp.zeros((64, 128), BF16)
    copies = [
        pltpu.make_async_copy(term_ref.at[pl.ds(8 * i, 8)], out_ref.at[pl.ds(8 * i, 8)], sems.at[i]) for i in range(4)
    ]
    for k in range(3):
        acts = gathered_acts(acts_ref, k)
        scale = scale_ref[k : k + 1, 0:1]
        terms = jnp.concatenate(
            [
                dot(acts[:, s * 256 : s * 256 + 256], rights[k][:, s * 256 : s * 256 + 256], CONTRACT_LAST)
                for s in range(2)
            ],
            axis=0,
        )
        for first in (0, 256, 512):
            width = min(256, 640 - first)
            block = terms[:, first : first + width]
            high = block.astype(BF16)
            low = (block - high.astype(F32)).astype(BF16)
            part = table[0:width, 0:width]
            rotated = dot(low, part) + dot(high, part)
            quantized = jnp.clip(rotated * scale, -127.0, 127.0).astype(BF16).astype(F32)
            total = quantized[0:128] + quantized[128:256]
            for b in range(first // 128, (first + width) // 128):
                half = total[:, b * 128 - first : b * 128 - first + 128].reshape(8, 2, 8, 128)
                if b < 4:
                    term_ref[k * 8 + b] = half[:, 0].reshape(64, 128).astype(BF16)
                    term_ref[k * 8 + 4 + b] = half[:, 1].reshape(64, 128).astype(BF16)
                else:
                    chosen = jnp.where(odd == 1, half[:, 1], half[:, 0])
                    term_ref[24 + k] = chosen.reshape(64, 128).astype(BF16)
        copies[k].start()
    copies[3].start()
    for copy in copies:
        copy.wait()


def resid_kernel(acts_ref, w_ref, xa_ref, inv_ref, gain_ref, _, near_ref, far_ref):
    _, odd, first = places()
    gain = feature_column(gain_ref, first, odd)
    inverse = inv_ref[0:1, :]
    tails = acts_ref[0, 96:104, :].astype(F32)
    for x in range(1, 4):
        tails = tails + acts_ref[x, 96:104, :].astype(F32)
    row_mean = tails[0:1] + tails[1:2] + tails[2:3]
    pair = jnp.concatenate([gathered_acts(acts_ref, k) for k in range(2)], axis=0)
    normed_grad = dot(w_ref[0:256], pair, CONTRACT_FIRST)
    unit = xa_ref[...].astype(F32) * inverse
    resid = inverse * (normed_grad * gain - unit * row_mean)
    main, half = own_rows(odd)
    shared_half = jnp.where(odd == 1, resid[576:640], resid[512:576])
    near_ref[main, :] = resid[0:512, 0:256]
    near_ref[half, :] = shared_half[:, 0:256]
    far_ref[main, :] = resid[0:512, 256:512].astype(BF16)
    far_ref[half, :] = shared_half[:, 256:512].astype(BF16)


def finish_kernel(g_ref, near_ref, far_ref, out_ref, done_ref):
    out_ref[...] = (g_ref[...].astype(F32) + (near_ref[...] + far_ref[...].astype(F32))).astype(BF16)
    done_ref[...] = jnp.zeros((8, 128), F32)


def total_kernel(terms_ref, _, share_ref):
    totals = []
    for yh in range(2):
        total = terms_ref[yh].astype(F32)
        for i in range(1, 32):
            total = total + terms_ref[2 * i + yh].astype(F32)
        totals.append(total)
    for x in range(4):
        both = jnp.concatenate([total[x * 8 : x * 8 + 8] for total in totals], axis=0).astype(BF16)
        for i in range(32):
            share_ref[i * 4 + x] = both


def received_rows(m):
    start = 8 * (2 * (m % 4) + m // 4)
    return slice(start, start + 8)


def restore_kernel(both_ref, sign_ref, table_ref, scale_ref, out_ref, held, sems):
    table = table_ref[0:128, 0:128]
    copies = []
    for k in range(3):
        factor = scale_ref[3 + k : 4 + k, :]
        for q in range(2):

            def put(block, low_half, high_half):
                sign = (2 * sign_ref[block : block + 1, :] - 1).astype(F32) * factor
                both = jnp.concatenate([low_half, high_half], axis=0) * sign
                held[k, 16 * q : 16 * q + 16, block * 128 : (block + 1) * 128] = both.astype(BF16)

            for b in range(4):
                halves = [dot(both_ref[q, k * 8 + 4 * i + b], table) for i in range(2)]
                for m in range(8):
                    rows = received_rows(m)
                    put(9 * (m // 2) + 5 * (m % 2) + b, halves[0][rows], halves[1][rows])
            shared = dot(both_ref[q, 24 + k], table)
            for p in range(4):
                put(9 * p + 4, shared[received_rows(2 * p)], shared[received_rows(2 * p + 1)])
        copy = pltpu.make_async_copy(held.at[k], out_ref.at[k], sems.at[k])
        copy.start()
        copies.append(copy)
    for copy in copies:
        copy.wait()


def call(kernel, outs, scalars=0, scratch=(), anywhere=(), out_space=pltpu.VMEM, limit=VMEM_LIMIT):
    def run(*operands):
        count = len(operands)
        spaces = [
            pltpu.SMEM if i >= count - scalars else pl.ANY if i in anywhere else pltpu.VMEM for i in range(count)
        ]
        return pl.pallas_call(
            kernel,
            out_shape=[jax.ShapeDtypeStruct(shape, dtype) for shape, dtype in outs],
            in_specs=[pl.BlockSpec(memory_space=place) for place in spaces],
            out_specs=[pl.BlockSpec(memory_space=out_space) for _ in outs],
            scratch_shapes=list(scratch),
            compiler_params=pltpu.CompilerParams(vmem_limit_bytes=limit),
            cost_estimate=pl.CostEstimate(flops=10**9, bytes_accessed=10**6, transcendentals=0),
            name=kernel.__name__,
        )(*operands)

    return run


def per_device(residual, out_grad, ffn_weights, norm_gain, exponents, sign_bits):
    gain = norm_gain.reshape(36, 128)
    signs = sign_bits.reshape(36, 128)
    table = jnp.asarray(np.kron(np.eye(2), signed_hadamard()), BF16)
    cores = [(0, 1), (1, 0)]
    x_cols, g_cols = residual.T, out_grad.T
    rows = ((640, 512), BF16)

    (send,) = call(
        prepare_kernel,
        [((8, 14, 16, 128), BF16)],
        scratch=[
            pltpu.VMEM((4, 3, 16, 1152), BF16),
            pltpu.VMEM((8, 14, 16, 128), BF16),
            pltpu.SemaphoreType.DMA((4,)),
            pltpu.SemaphoreType.DMA((8,)),
        ],
        anywhere=(0,),
        out_space=pl.ANY,
        limit=60 * 1024 * 1024,
    )(ffn_weights)
    received = lax.all_to_all(send.reshape(8, 224, 128), AXES, 0, 0, axis_index_groups=near_groups())
    near_x, near_g, _ = lax.optimization_barrier((x_cols, g_cols, send))
    (near,) = call(join_kernel, [((1152, 256), BF16)])(near_x, near_g)
    far = lax.ppermute(near, "c", cores)
    xa, ga, half, tail, scales = call(
        align_kernel, [rows, rows, ((128, 512), BF16), ((8, 512), BF16), ((8, 128), F32)], scalars=1
    )(near, far, exponents)
    other_half = lax.ppermute(half, "x", [(0, 1), (1, 0), (2, 3), (3, 2)])
    parts, weights = call(forward_kernel, [((4, 104, 512), BF16), ((384, 640), BF16)], anywhere=(5,))(
        received.reshape(8, 14, 16, 128), xa, ga, tail, gain, other_half
    )

    parts = lax.all_to_all(parts, "x", 0, 0)
    sums, own = call(sum_kernel, [((104, 512), BF16), ((96, 512), F32)])(parts)
    sums = lax.all_gather(sums, "yh", axis=0)
    message, inverse = call(activation_kernel, [((4, 104, 512), BF16), ((8, 512), F32)])(sums, own)
    acts = lax.all_to_all(message, "x", 0, 0)
    (terms,) = call(
        gradient_kernel,
        [((32, 64, 128), BF16)],
        scratch=[pltpu.VMEM((32, 64, 128), BF16), pltpu.SemaphoreType.DMA((4,))],
        out_space=pl.ANY,
    )(acts, xa, ga, other_half, inverse, gain, signs, table, scales)

    summands = lax.all_to_all(terms.reshape(64, 32, 128), ("z", "yl", "yh"), 0, 0)
    near_resid, far_resid = call(resid_kernel, [((576, 256), F32), ((576, 256), BF16)], anywhere=(5,))(
        acts, weights, xa, inverse, gain, terms
    )
    far_resid = lax.ppermute(far_resid, "c", cores)
    resid_cols, done = call(finish_kernel, [((576, 256), BF16), ((8, 128), F32)])(g_cols, near_resid, far_resid)
    (share,) = call(total_kernel, [((128, 16, 128), BF16)])(summands, done)
    share = lax.all_to_all(share, ("z", "yl", "x"), 0, 0).reshape(32, 64, 128)
    both = lax.all_gather(share[0:27], "c", axis=0)
    (weight_grads,) = call(
        restore_kernel,
        [((3, 32, 4608), BF16)],
        scratch=[pltpu.VMEM((3, 32, 4608), BF16), pltpu.SemaphoreType.DMA((3,))],
        out_space=pl.ANY,
    )(both, signs, table, scales)
    return (resid_cols.T, weight_grads)


def near_groups():
    def flat(z, yl, c, yh, x):
        return (((z * 4 + yl) * 2 + c) * 2 + yh) * 4 + x

    return [
        [flat(z, 3 - yl if yh else yl, c, yh, x) for yh in range(2) for x in range(4)]
        for z in range(8)
        for yl in range(4)
        for c in range(2)
    ]


def solution(mesh):
    fine = Mesh(mesh.devices.reshape(8, 4, 2, 2, 4), AXES)
    rows = P(DP, MP)
    return jax.shard_map(
        per_device,
        mesh=fine,
        in_specs=(rows, rows, P(None, MP, None), P(), P(), P()),
        out_specs=(rows, P(None, MP, None)),
        check_vma=False,
    )
```

```python
import functools

import jax
import jax.numpy as jnp
import numpy as np
from jax import lax
from jax.experimental import pallas as pl
from jax.experimental.pallas import tpu as pltpu
from jax.sharding import Mesh
from jax.sharding import PartitionSpec as P

F32 = jnp.float32
BF16 = jnp.bfloat16
AXES = ("z", "yl", "c", "yh", "x")
DP = ("z", "yl", "c")
MP = ("yh", "x")
VMEM_LIMIT = 20 * 1024 * 1024
FEATURES = 4608
CONTRACT_LAST = (((1,), (1,)), ((), ()))
CONTRACT_FIRST = (((0,), (0,)), ((), ()))


def signed_hadamard():
    table = np.array([[1.0]], np.float32)
    for _ in range(7):
        table = np.block([[table, table], [table, -table]])
    return table


def gelu_parts(values):
    tanh_input = 0.7978845608 * (values + 0.044715 * values * values * values)
    tanhed = jnp.tanh(tanh_input)
    forward = 0.5 * values * (1.0 + tanhed)
    gelu_slope = 0.5 * (1.0 + tanhed) + 0.5 * values * (1.0 - tanhed * tanhed) * 0.7978845608 * (
        1.0 + 3.0 * 0.044715 * values * values
    )
    return (forward, gelu_slope)


def pieces(values):
    high = values.astype(BF16)
    rest = values - high.astype(F32)
    middle = rest.astype(BF16)
    low = (rest - middle.astype(F32)).astype(BF16)
    return (high, middle, low)


def dot(left, right, dims=(((1,), (0,)), ((), ()))):
    return lax.dot_general(left, right, dims, preferred_element_type=F32)


def places():
    odd = lax.axis_index("x") % 2
    pair = lax.axis_index("yh") * 2 + lax.axis_index("x") // 2
    return (lax.axis_index("c"), odd, pair * 9)


def local_rows(table_ref, first, odd):
    return [table_ref[pl.ds(first + 5 * odd + b, 1), :] for b in range(4)] + [table_ref[pl.ds(first + 4, 1), :]]


def own_rows(odd):
    return (
        pl.ds(pl.multiple_of(odd * 64, 64), 512),
        pl.ds(pl.multiple_of((1 - odd) * 512, 64), 64),
    )


def prepare_kernel(w_ref, send_ref, held, packed, in_sems, out_sems):
    core, _, _ = places()
    rows = pl.ds(pl.multiple_of(core * 16, 16), 16)
    loads = [
        pltpu.make_async_copy(w_ref.at[:, rows, pl.ds(p * 1152, 1152)], held.at[p], in_sems.at[p]) for p in range(4)
    ]
    for load in loads:
        load.start()
    lane = lax.broadcasted_iota(jnp.int32, (16, 128), 1)
    stores = []
    for m in range(8):
        pair, odd = m // 2, m % 2
        if odd == 0:
            loads[pair].wait()
        for b in range(4):
            column = (5 * odd + b) * 128
            for k in range(3):
                packed[m, b * 3 + k] = held[pair, k, :, column : column + 128]
        gate, up, down = [held[pair, k, :, 512:640] for k in range(3)]
        turned = pltpu.roll(up.astype(F32), 64, 1)
        packed[m, 12] = jnp.where((lane >= 64) == (odd == 1), gate.astype(F32), turned).astype(BF16)
        packed[m, 13] = down
        store = pltpu.make_async_copy(packed.at[m], send_ref.at[m], out_sems.at[m])
        store.start()
        stores.append(store)
    for store in stores:
        store.wait()


def join_kernel(x_ref, g_ref, out_ref, half_ref):
    _, odd, _ = places()
    half = pl.ds(pl.multiple_of((1 - odd) * 512, 64), 64)
    out_ref[0:576, :] = x_ref[...]
    out_ref[576:1152, :] = g_ref[...]
    half_ref[0:64, :] = x_ref[half, :]
    half_ref[64:128, :] = g_ref[half, :]


def align_kernel(near_ref, far_ref, exps_ref, xa_ref, ga_ref, tail_ref, scale_ref):
    place = lax.broadcasted_iota(jnp.int32, (8, 128), 0)
    scales = jnp.zeros((8, 128), F32)
    for k in range(3):
        e = exps_ref[k]
        up = jnp.where(e == 3, 8.0, jnp.where(e == 4, 16.0, jnp.where(e == 5, 32.0, 64.0)))
        down = jnp.where(e == 3, 2.0**-9, jnp.where(e == 4, 2.0**-10, jnp.where(e == 5, 2.0**-11, 2.0**-12)))
        scales = jnp.where(place == k, up, jnp.where(place == 3 + k, down, scales))
    scale_ref[...] = scales * float(128.0**-0.5)
    _, odd, _ = places()
    main, half = pl.multiple_of(odd * 64, 64), pl.multiple_of((1 - odd) * 512, 64)
    mine = pl.ds(pl.multiple_of(512 + odd * 64, 64), 64)
    theirs = pl.ds(pl.multiple_of(576 - odd * 64, 64), 64)
    for part, to_ref in enumerate((xa_ref, ga_ref)):
        for side, ref in enumerate((near_ref, far_ref)):
            tokens = pl.ds(side * 256, 256)
            to_ref[0:512, tokens] = ref[pl.ds(576 * part + main, 512), :]
            to_ref[mine, tokens] = ref[pl.ds(576 * part + half, 64), :]
            to_ref[theirs, tokens] = jnp.zeros((64, 256), BF16)
    wide = xa_ref[...].astype(F32)
    tail_ref[...] = stacked_pieces(jnp.sum(wide * wide, axis=0, keepdims=True))


def forward_kernel(recv_ref, xa_ref, ga_ref, tail_ref, gain_ref, _near, _far, part_ref, own_ref, w_ref):
    _, odd, first = places()
    for j in range(8):
        for k in range(3):
            rows = slice(k * 128 + j * 16, k * 128 + j * 16 + 16)
            for b in range(4):
                w_ref[rows, b * 128 : (b + 1) * 128] = recv_ref[j, b * 3 + k]
        w_ref[j * 16 : j * 16 + 16, 512:640] = recv_ref[j, 12]
        w_ref[128 + j * 16 : 128 + j * 16 + 16, 512:640] = pltpu.roll(recv_ref[j, 12].astype(F32), 64, 1).astype(BF16)
        w_ref[256 + j * 16 : 256 + j * 16 + 16, 512:640] = recv_ref[j, 13]
    gained = w_ref[0:256].astype(F32) * jnp.concatenate(local_rows(gain_ref, first, odd), axis=1)
    high = gained.astype(BF16)
    low = (gained - high.astype(F32)).astype(BF16)
    both = dot(jnp.concatenate([low, high], axis=0), xa_ref[...])
    gate_up = both[0:256] + both[256:512]
    down = dot(w_ref[256:384], ga_ref[...])
    tail = tail_ref[...]
    my_x = lax.axis_index("x")
    for yh in range(2):
        for k, source in enumerate((gate_up[0:128], gate_up[128:256], down)):
            rows = slice(yh * 48 + k * 16, yh * 48 + k * 16 + 16)
            own = jnp.zeros((16, 512), F32)
            for x in range(4):
                j = 4 * yh + x
                values = source[j * 16 : j * 16 + 16]
                part_ref[x, rows, :] = values.astype(BF16)
                own = jnp.where(my_x == x, values, own)
            own_ref[rows, :] = own
    for x in range(4):
        part_ref[x, 96:104, :] = tail


def stacked_pieces(row):
    place = lax.broadcasted_iota(jnp.int32, (8, 512), 0)
    tail = jnp.zeros((8, 512), F32)
    for i, piece in enumerate(pieces(row)):
        tail = jnp.where(place == i, piece.astype(F32), tail)
    return tail.astype(BF16)


def sum_kernel(parts_ref, mine_ref, out_ref, own_ref):
    my_x = lax.axis_index("x")
    total = mine_ref[...]
    tails = jnp.zeros((8, 512), F32)
    for i in range(4):
        total = total + jnp.where(my_x == i, 0.0, parts_ref[i, 0:96, :].astype(F32))
        tails = tails + parts_ref[i, 96:104, :].astype(F32)
    own_ref[...] = total
    out_ref[0:96, :] = total.astype(BF16)
    out_ref[96:104, :] = stacked_pieces(tails[0:1] + tails[1:2] + tails[2:3])


def activation_kernel(parts_ref, own_ref, out_ref, inv_ref):
    high = lax.axis_index("yh") == 1
    tails = parts_ref[0, 96:104, :].astype(F32) + parts_ref[1, 96:104, :].astype(F32)
    sums = tails[0:1] + tails[1:2] + tails[2:3]
    inverse = lax.rsqrt(sums / FEATURES + 1e-06)
    inv_ref[...] = jnp.broadcast_to(inverse, (8, 512))
    others = [parts_ref[i, 0:96, :].astype(F32) for i in range(2)]
    total = own_ref[...] + jnp.where(high, others[0], others[1])
    mean = jnp.zeros((1, 512), F32)
    for yh in range(2):
        start = yh * 48
        gate_pre = total[start : start + 16] * inverse
        up_proj = total[start + 16 : start + 32] * inverse
        hidden_grad = total[start + 32 : start + 48]
        activated, slope = gelu_parts(gate_pre)
        hidden = (activated * up_proj).astype(BF16)
        gate_grad = (hidden_grad * up_proj * slope).astype(BF16)
        up_grad = (hidden_grad * activated).astype(BF16)
        products = gate_grad.astype(F32) * gate_pre + up_grad.astype(F32) * up_proj
        mean = mean + jnp.sum(products, axis=0, keepdims=True) / FEATURES
        for i in range(4):
            out_ref[i, start : start + 16, :] = gate_grad
            out_ref[i, start + 16 : start + 32, :] = up_grad
            out_ref[i, start + 32 : start + 48, :] = hidden
    tail = stacked_pieces(mean)
    for i in range(4):
        out_ref[i, 96:104, :] = tail


def feature_column(table_ref, first, odd):
    diagonal = lax.broadcasted_iota(jnp.int32, (128, 128), 0) == lax.broadcasted_iota(jnp.int32, (128, 128), 1)
    rows = local_rows(table_ref, first, odd)
    return jnp.concatenate(
        [jnp.sum(jnp.where(diagonal, row.astype(F32), 0.0), axis=1, keepdims=True) for row in rows], axis=0
    )


def gathered_acts(acts_ref, k):
    starts = [(j % 4, j // 4 * 48 + k * 16) for j in range(8)]
    return jnp.concatenate([acts_ref[x, start : start + 16, :] for x, start in starts], axis=0)


def gradient_kernel(
    acts_ref, xa_ref, ga_ref, near_half_ref, far_half_ref, inv_ref, gain_ref, sign_ref, table_ref, scale_ref, out_ref, term_ref, sems
):
    _, odd, first_block = places()
    table = table_ref[...]
    sign = 2.0 * feature_column(sign_ref, first_block, odd) - 1.0
    gain = feature_column(gain_ref, first_block, odd) * sign
    theirs = (lax.broadcasted_iota(jnp.int32, (128, 512), 0) >= 64) == (odd == 0)
    rights = []
    for part, (ref, factor) in enumerate(((xa_ref, inv_ref[0:1, :]), (ga_ref, None))):
        other = jnp.concatenate(
            [half_ref[part * 64 : part * 64 + 64, :] for half_ref in (near_half_ref, far_half_ref)], axis=1
        ).astype(F32)
        shared = jnp.where(theirs, jnp.concatenate([other, other], axis=0), ref[512:640, :].astype(F32))
        values = jnp.concatenate([ref[0:512, :].astype(F32), shared], axis=0)
        rights.append((values * sign if factor is None else values * factor * gain).astype(BF16))
    for s in range(27, 32):
        term_ref[s] = jnp.zeros((64, 128), BF16)
    copies = []

    def send(at, count):
        copy = pltpu.make_async_copy(term_ref.at[pl.ds(at, count)], out_ref.at[pl.ds(at, count)], sems.at[len(copies)])
        copy.start()
        copies.append(copy)

    for matrices, right in (((0, 1), rights[0]), ((2,), rights[1])):
        acts = jnp.concatenate([gathered_acts(acts_ref, k) for k in matrices], axis=0)
        height = acts.shape[0]
        terms = jnp.concatenate(
            [
                dot(acts[:, s * 256 : s * 256 + 256], right[:, s * 256 : s * 256 + 256], CONTRACT_LAST)
                for s in range(2)
            ],
            axis=0,
        )
        for first in (512, 0, 256):
            width = min(256, 640 - first)
            block = terms[:, first : first + width]
            high = block.astype(BF16)
            low = (block - high.astype(F32)).astype(BF16)
            part = table[0:width, 0:width]
            rotated = dot(low, part) + dot(high, part)
            for i, k in enumerate(matrices):
                scale = scale_ref[k : k + 1, 0:1]
                total = None
                for start in (i * 128, height + i * 128):
                    scaled = jnp.clip(rotated[start : start + 128] * scale, -127.0, 127.0)
                    quantized = scaled.astype(BF16).astype(F32)
                    total = quantized if total is None else total + quantized
                for b in range(first // 128, (first + width) // 128):
                    half = total[:, b * 128 - first : b * 128 - first + 128].reshape(8, 2, 8, 128)
                    if b < 4:
                        term_ref[k * 8 + b] = half[:, 0].reshape(64, 128).astype(BF16)
                        term_ref[k * 8 + 4 + b] = half[:, 1].reshape(64, 128).astype(BF16)
                    else:
                        chosen = jnp.where(odd == 1, half[:, 1], half[:, 0])
                        term_ref[24 + k] = chosen.reshape(64, 128).astype(BF16)
                if first < 512:
                    send(k * 8 + first // 128, 2)
                    send(k * 8 + 4 + first // 128, 2)
                elif k == 2:
                    send(24, 8)
    for copy in copies:
        copy.wait()


def resid_kernel(acts_ref, w_ref, xa_ref, inv_ref, gain_ref, _, near_ref, far_ref):
    _, odd, first = places()
    gain = feature_column(gain_ref, first, odd)
    inverse = inv_ref[0:1, :]
    tails = acts_ref[0, 96:104, :].astype(F32)
    for x in range(1, 4):
        tails = tails + acts_ref[x, 96:104, :].astype(F32)
    row_mean = tails[0:1] + tails[1:2] + tails[2:3]
    pair = jnp.concatenate([gathered_acts(acts_ref, k) for k in range(2)], axis=0)
    normed_grad = dot(w_ref[0:256], pair, CONTRACT_FIRST)
    unit = xa_ref[...].astype(F32) * inverse
    resid = inverse * (normed_grad * gain - unit * row_mean)
    main, half = own_rows(odd)
    shared_half = jnp.where(odd == 1, resid[576:640], resid[512:576])
    near_ref[main, :] = resid[0:512, 0:256]
    near_ref[half, :] = shared_half[:, 0:256]
    far_ref[main, :] = resid[0:512, 256:512].astype(BF16)
    far_ref[half, :] = shared_half[:, 256:512].astype(BF16)


def finish_kernel(g_ref, near_ref, far_ref, out_ref, done_ref):
    out_ref[...] = (g_ref[...].astype(F32) + (near_ref[...] + far_ref[...].astype(F32))).astype(BF16)
    done_ref[...] = jnp.zeros((8, 128), F32)


def total_kernel(terms_ref, _, share_ref):
    totals = []
    for yh in range(2):
        total = terms_ref[yh].astype(F32)
        for i in range(1, 32):
            total = total + terms_ref[2 * i + yh].astype(F32)
        totals.append(total)
    for x in range(4):
        both = jnp.concatenate([total[x * 8 : x * 8 + 8] for total in totals], axis=0).astype(BF16)
        for i in range(32):
            share_ref[i * 4 + x] = both


def received_rows(m):
    start = 8 * (2 * (m % 4) + m // 4)
    return slice(start, start + 8)


def restore_kernel(both_ref, sign_ref, table_ref, scale_ref, out_ref, held, sems):
    table = table_ref[0:128, 0:128]
    copies = []
    for k in range(3):
        factor = scale_ref[3 + k : 4 + k, :]
        for q in range(2):

            def put(block, low_half, high_half):
                sign = (2 * sign_ref[block : block + 1, :] - 1).astype(F32) * factor
                both = jnp.concatenate([low_half, high_half], axis=0) * sign
                held[k, 16 * q : 16 * q + 16, block * 128 : (block + 1) * 128] = both.astype(BF16)

            own = dot(both_ref[q, k * 8 : k * 8 + 8].reshape(512, 128), table)
            for b in range(4):
                halves = [own[(4 * i + b) * 64 : (4 * i + b) * 64 + 64] for i in range(2)]
                for m in range(8):
                    rows = received_rows(m)
                    put(9 * (m // 2) + 5 * (m % 2) + b, halves[0][rows], halves[1][rows])
            shared = dot(both_ref[q, 24 + k], table)
            for p in range(4):
                put(9 * p + 4, shared[received_rows(2 * p)], shared[received_rows(2 * p + 1)])
        copy = pltpu.make_async_copy(held.at[k], out_ref.at[k], sems.at[k])
        copy.start()
        copies.append(copy)
    for copy in copies:
        copy.wait()


def call(kernel, outs, scalars=0, scratch=(), anywhere=(), out_space=pltpu.VMEM, limit=VMEM_LIMIT):
    def run(*operands):
        count = len(operands)
        spaces = [
            pltpu.SMEM if i >= count - scalars else pl.ANY if i in anywhere else pltpu.VMEM for i in range(count)
        ]
        return pl.pallas_call(
            kernel,
            out_shape=[jax.ShapeDtypeStruct(shape, dtype) for shape, dtype in outs],
            in_specs=[pl.BlockSpec(memory_space=place) for place in spaces],
            out_specs=[pl.BlockSpec(memory_space=out_space) for _ in outs],
            scratch_shapes=list(scratch),
            compiler_params=pltpu.CompilerParams(vmem_limit_bytes=limit),
            cost_estimate=pl.CostEstimate(flops=10**9, bytes_accessed=10**6, transcendentals=0),
            name=kernel.__name__,
        )(*operands)

    return run


def per_device(residual, out_grad, ffn_weights, norm_gain, exponents, sign_bits):
    gain = norm_gain.reshape(36, 128)
    signs = sign_bits.reshape(36, 128)
    table = jnp.asarray(np.kron(np.eye(2), signed_hadamard()), BF16)
    cores = [(0, 1), (1, 0)]
    x_cols, g_cols = residual.T, out_grad.T
    rows = ((640, 512), BF16)

    (send,) = call(
        prepare_kernel,
        [((8, 14, 16, 128), BF16)],
        scratch=[
            pltpu.VMEM((4, 3, 16, 1152), BF16),
            pltpu.VMEM((8, 14, 16, 128), BF16),
            pltpu.SemaphoreType.DMA((4,)),
            pltpu.SemaphoreType.DMA((8,)),
        ],
        anywhere=(0,),
        out_space=pl.ANY,
        limit=60 * 1024 * 1024,
    )(ffn_weights)
    received = lax.all_to_all(send.reshape(8, 224, 128), AXES, 0, 0, axis_index_groups=near_groups())
    near_x, near_g, _ = lax.optimization_barrier((x_cols, g_cols, send))
    near, half = call(join_kernel, [((1152, 256), BF16), ((128, 256), BF16)])(near_x, near_g)
    far = lax.ppermute(near, "c", cores)
    near_half = lax.ppermute(half, "x", [(0, 1), (1, 0), (2, 3), (3, 2)])
    across = [(c * 4 + x, (1 - c) * 4 + (x ^ 1)) for c in range(2) for x in range(4)]
    far_half = lax.ppermute(half, ("c", "x"), across)
    xa, ga, tail, scales = call(align_kernel, [rows, rows, ((8, 512), BF16), ((8, 128), F32)], scalars=1)(
        near, far, exponents
    )
    parts, mine, weights = call(
        forward_kernel, [((4, 104, 512), BF16), ((96, 512), F32), ((384, 640), BF16)], anywhere=(5, 6)
    )(
        received.reshape(8, 14, 16, 128), xa, ga, tail, gain, near_half, far_half
    )

    parts = lax.all_to_all(parts, "x", 0, 0)
    sums, own = call(sum_kernel, [((104, 512), BF16), ((96, 512), F32)])(parts, mine)
    sums = lax.all_gather(sums, "yh", axis=0)
    message, inverse = call(activation_kernel, [((4, 104, 512), BF16), ((8, 512), F32)])(sums, own)
    acts = lax.all_to_all(message, "x", 0, 0)
    (terms,) = call(
        gradient_kernel,
        [((32, 64, 128), BF16)],
        scratch=[pltpu.VMEM((32, 64, 128), BF16), pltpu.SemaphoreType.DMA((13,))],
        out_space=pl.ANY,
    )(acts, xa, ga, near_half, far_half, inverse, gain, signs, table, scales)

    summands = lax.all_to_all(terms.reshape(64, 32, 128), ("z", "yl", "yh"), 0, 0)
    near_resid, far_resid = call(resid_kernel, [((576, 256), F32), ((576, 256), BF16)], anywhere=(5,))(
        acts, weights, xa, inverse, gain, terms
    )
    far_resid = lax.ppermute(far_resid, "c", cores)
    resid_cols, done = call(finish_kernel, [((576, 256), BF16), ((8, 128), F32)])(g_cols, near_resid, far_resid)
    (share,) = call(total_kernel, [((128, 16, 128), BF16)])(summands, done)
    share = lax.all_to_all(share, ("z", "yl", "x"), 0, 0).reshape(32, 64, 128)
    both = lax.all_gather(share[0:27], "c", axis=0)
    (weight_grads,) = call(
        restore_kernel,
        [((3, 32, 4608), BF16)],
        scratch=[pltpu.VMEM((3, 32, 4608), BF16), pltpu.SemaphoreType.DMA((3,))],
        out_space=pl.ANY,
    )(both, signs, table, scales)
    return (resid_cols.T, weight_grads)


def near_groups():
    def flat(z, yl, c, yh, x):
        return (((z * 4 + yl) * 2 + c) * 2 + yh) * 4 + x

    return [
        [flat(z, 3 - yl if yh else yl, c, yh, x) for yh in range(2) for x in range(4)]
        for z in range(8)
        for yl in range(4)
        for c in range(2)
    ]


def solution(mesh):
    fine = Mesh(mesh.devices.reshape(8, 4, 2, 2, 4), AXES)
    rows = P(DP, MP)
    return jax.shard_map(
        per_device,
        mesh=fine,
        in_specs=(rows, rows, P(None, MP, None), P(), P(), P()),
        out_specs=(rows, P(None, MP, None)),
        check_vma=False,
    )
```

```python
import functools

import jax
import jax.numpy as jnp
import numpy as np
from jax import lax
from jax.experimental import pallas as pl
from jax.experimental.pallas import tpu as pltpu
from jax.sharding import Mesh
from jax.sharding import PartitionSpec as P

F32 = jnp.float32
BF16 = jnp.bfloat16
AXES = ("z", "yl", "c", "yh", "x")
DP = ("z", "yl", "c")
MP = ("yh", "x")
VMEM_LIMIT = 20 * 1024 * 1024
FEATURES = 4608
CONTRACT_LAST = (((1,), (1,)), ((), ()))
CONTRACT_FIRST = (((0,), (0,)), ((), ()))


def signed_hadamard():
    table = np.array([[1.0]], np.float32)
    for _ in range(7):
        table = np.block([[table, table], [table, -table]])
    return table


def gelu_parts(values):
    tanh_input = 0.7978845608 * (values + 0.044715 * values * values * values)
    tanhed = jnp.tanh(tanh_input)
    forward = 0.5 * values * (1.0 + tanhed)
    gelu_slope = 0.5 * (1.0 + tanhed) + 0.5 * values * (1.0 - tanhed * tanhed) * 0.7978845608 * (
        1.0 + 3.0 * 0.044715 * values * values
    )
    return (forward, gelu_slope)


def pieces(values):
    high = values.astype(BF16)
    rest = values - high.astype(F32)
    middle = rest.astype(BF16)
    low = (rest - middle.astype(F32)).astype(BF16)
    return (high, middle, low)


def dot(left, right, dims=(((1,), (0,)), ((), ()))):
    return lax.dot_general(left, right, dims, preferred_element_type=F32)


def places():
    odd = lax.axis_index("x") % 2
    pair = lax.axis_index("yh") * 2 + lax.axis_index("x") // 2
    return (lax.axis_index("c"), odd, pair * 9)


def local_rows(table_ref, first, odd):
    return [table_ref[pl.ds(first + 5 * odd + b, 1), :] for b in range(4)] + [table_ref[pl.ds(first + 4, 1), :]]


def own_rows(odd):
    return (
        pl.ds(pl.multiple_of(odd * 64, 64), 512),
        pl.ds(pl.multiple_of((1 - odd) * 512, 64), 64),
    )


def prepare_kernel(w_ref, send_ref, held, packed, in_sems, out_sems):
    core, _, _ = places()
    rows = pl.ds(pl.multiple_of(core * 16, 16), 16)
    loads = [
        pltpu.make_async_copy(w_ref.at[:, rows, pl.ds(p * 1152, 1152)], held.at[p], in_sems.at[p]) for p in range(4)
    ]
    for load in loads:
        load.start()
    lane = lax.broadcasted_iota(jnp.int32, (16, 128), 1)
    stores = []
    for m in range(8):
        pair, odd = m // 2, m % 2
        if odd == 0:
            loads[pair].wait()
        for b in range(4):
            column = (5 * odd + b) * 128
            for k in range(3):
                packed[m, b * 3 + k] = held[pair, k, :, column : column + 128]
        gate, up, down = [held[pair, k, :, 512:640] for k in range(3)]
        turned = pltpu.roll(up.astype(F32), 64, 1)
        packed[m, 12] = jnp.where((lane >= 64) == (odd == 1), gate.astype(F32), turned).astype(BF16)
        packed[m, 13] = down
        store = pltpu.make_async_copy(packed.at[m], send_ref.at[m], out_sems.at[m])
        store.start()
        stores.append(store)
    for store in stores:
        store.wait()


def join_kernel(x_ref, g_ref, out_ref):
    out_ref[0:576, :] = x_ref[...]
    out_ref[576:1152, :] = g_ref[...]


def align_kernel(near_ref, far_ref, exps_ref, xa_ref, ga_ref, half_ref, tail_ref, scale_ref):
    place = lax.broadcasted_iota(jnp.int32, (8, 128), 0)
    scales = jnp.zeros((8, 128), F32)
    for k in range(3):
        e = exps_ref[k]
        up = jnp.where(e == 3, 8.0, jnp.where(e == 4, 16.0, jnp.where(e == 5, 32.0, 64.0)))
        down = jnp.where(e == 3, 2.0**-9, jnp.where(e == 4, 2.0**-10, jnp.where(e == 5, 2.0**-11, 2.0**-12)))
        scales = jnp.where(place == k, up, jnp.where(place == 3 + k, down, scales))
    scale_ref[...] = scales * float(128.0**-0.5)
    _, odd, _ = places()
    main, half = pl.multiple_of(odd * 64, 64), pl.multiple_of((1 - odd) * 512, 64)
    mine = pl.ds(pl.multiple_of(512 + odd * 64, 64), 64)
    theirs = pl.ds(pl.multiple_of(576 - odd * 64, 64), 64)
    for part, to_ref in enumerate((xa_ref, ga_ref)):
        for side, ref in enumerate((near_ref, far_ref)):
            tokens = pl.ds(side * 256, 256)
            to_ref[0:512, tokens] = ref[pl.ds(576 * part + main, 512), :]
            rows = ref[pl.ds(576 * part + half, 64), :]
            half_ref[pl.ds(64 * part, 64), tokens] = rows
            to_ref[mine, tokens] = rows
            to_ref[theirs, tokens] = jnp.zeros((64, 256), BF16)
    wide = xa_ref[...].astype(F32)
    tail_ref[...] = stacked_pieces(jnp.sum(wide * wide, axis=0, keepdims=True))


def forward_kernel(recv_ref, xa_ref, ga_ref, tail_ref, gain_ref, _, part_ref, own_ref, w_ref):
    _, odd, first = places()
    for j in range(8):
        for k in range(3):
            rows = slice(k * 128 + j * 16, k * 128 + j * 16 + 16)
            for b in range(4):
                w_ref[rows, b * 128 : (b + 1) * 128] = recv_ref[j, b * 3 + k]
        w_ref[j * 16 : j * 16 + 16, 512:640] = recv_ref[j, 12]
        w_ref[128 + j * 16 : 128 + j * 16 + 16, 512:640] = pltpu.roll(recv_ref[j, 12].astype(F32), 64, 1).astype(BF16)
        w_ref[256 + j * 16 : 256 + j * 16 + 16, 512:640] = recv_ref[j, 13]
    gained = w_ref[0:256].astype(F32) * jnp.concatenate(local_rows(gain_ref, first, odd), axis=1)
    high = gained.astype(BF16)
    low = (gained - high.astype(F32)).astype(BF16)
    both = dot(jnp.concatenate([low, high], axis=0), xa_ref[...])
    gate_up = both[0:256] + both[256:512]
    down = dot(w_ref[256:384], ga_ref[...])
    tail = tail_ref[...]
    my_x = lax.axis_index("x")
    for yh in range(2):
        for k, source in enumerate((gate_up[0:128], gate_up[128:256], down)):
            rows = slice(yh * 48 + k * 16, yh * 48 + k * 16 + 16)
            own = jnp.zeros((16, 512), F32)
            for x in range(4):
                j = 4 * yh + x
                values = source[j * 16 : j * 16 + 16]
                part_ref[x, rows, :] = values.astype(BF16)
                own = jnp.where(my_x == x, values, own)
            own_ref[rows, :] = own
    for x in range(4):
        part_ref[x, 96:104, :] = tail


def stacked_pieces(row):
    place = lax.broadcasted_iota(jnp.int32, (8, 512), 0)
    tail = jnp.zeros((8, 512), F32)
    for i, piece in enumerate(pieces(row)):
        tail = jnp.where(place == i, piece.astype(F32), tail)
    return tail.astype(BF16)


def sum_kernel(parts_ref, mine_ref, out_ref, own_ref):
    my_x = lax.axis_index("x")
    total = mine_ref[...]
    tails = jnp.zeros((8, 512), F32)
    for i in range(4):
        total = total + jnp.where(my_x == i, 0.0, parts_ref[i, 0:96, :].astype(F32))
        tails = tails + parts_ref[i, 96:104, :].astype(F32)
    own_ref[...] = total
    out_ref[0:96, :] = total.astype(BF16)
    out_ref[96:104, :] = stacked_pieces(tails[0:1] + tails[1:2] + tails[2:3])


def activation_kernel(parts_ref, own_ref, out_ref, inv_ref):
    high = lax.axis_index("yh") == 1
    tails = parts_ref[0, 96:104, :].astype(F32) + parts_ref[1, 96:104, :].astype(F32)
    sums = tails[0:1] + tails[1:2] + tails[2:3]
    inverse = lax.rsqrt(sums / FEATURES + 1e-06)
    inv_ref[...] = jnp.broadcast_to(inverse, (8, 512))
    others = [parts_ref[i, 0:96, :].astype(F32) for i in range(2)]
    total = own_ref[...] + jnp.where(high, others[0], others[1])
    mean = jnp.zeros((1, 512), F32)
    for yh in range(2):
        start = yh * 48
        gate_pre = total[start : start + 16] * inverse
        up_proj = total[start + 16 : start + 32] * inverse
        hidden_grad = total[start + 32 : start + 48]
        activated, slope = gelu_parts(gate_pre)
        hidden = (activated * up_proj).astype(BF16)
        gate_grad = (hidden_grad * up_proj * slope).astype(BF16)
        up_grad = (hidden_grad * activated).astype(BF16)
        products = gate_grad.astype(F32) * gate_pre + up_grad.astype(F32) * up_proj
        mean = mean + jnp.sum(products, axis=0, keepdims=True) / FEATURES
        for i in range(4):
            out_ref[i, start : start + 16, :] = gate_grad
            out_ref[i, start + 16 : start + 32, :] = up_grad
            out_ref[i, start + 32 : start + 48, :] = hidden
    tail = stacked_pieces(mean)
    for i in range(4):
        out_ref[i, 96:104, :] = tail


def feature_column(table_ref, first, odd):
    diagonal = lax.broadcasted_iota(jnp.int32, (128, 128), 0) == lax.broadcasted_iota(jnp.int32, (128, 128), 1)
    rows = local_rows(table_ref, first, odd)
    return jnp.concatenate(
        [jnp.sum(jnp.where(diagonal, row.astype(F32), 0.0), axis=1, keepdims=True) for row in rows], axis=0
    )


def gathered_acts(acts_ref, k):
    starts = [(j % 4, j // 4 * 48 + k * 16) for j in range(8)]
    return jnp.concatenate([acts_ref[x, start : start + 16, :] for x, start in starts], axis=0)


def gradient_kernel(
    acts_ref, xa_ref, ga_ref, half_ref, inv_ref, gain_ref, sign_ref, table_ref, scale_ref, out_ref, term_ref, sems
):
    _, odd, first_block = places()
    table = table_ref[...]
    sign = 2.0 * feature_column(sign_ref, first_block, odd) - 1.0
    gain = feature_column(gain_ref, first_block, odd) * sign
    theirs = (lax.broadcasted_iota(jnp.int32, (128, 512), 0) >= 64) == (odd == 0)
    rights = []
    for part, (ref, factor) in enumerate(((xa_ref, inv_ref[0:1, :]), (ga_ref, None))):
        other = half_ref[part * 64 : part * 64 + 64, :].astype(F32)
        shared = jnp.where(theirs, jnp.concatenate([other, other], axis=0), ref[512:640, :].astype(F32))
        values = jnp.concatenate([ref[0:512, :].astype(F32), shared], axis=0)
        rights.append((values * sign if factor is None else values * factor * gain).astype(BF16))
    for s in range(27, 32):
        term_ref[s] = jnp.zeros((64, 128), BF16)
    copies = []

    def send(at, count):
        copy = pltpu.make_async_copy(term_ref.at[pl.ds(at, count)], out_ref.at[pl.ds(at, count)], sems.at[len(copies)])
        copy.start()
        copies.append(copy)

    for matrices, right in (((2,), rights[1]), ((0, 1), rights[0])):
        acts = jnp.concatenate([gathered_acts(acts_ref, k) for k in matrices], axis=0)
        height = acts.shape[0]
        terms = jnp.concatenate(
            [
                dot(acts[:, s * 256 : s * 256 + 256], right[:, s * 256 : s * 256 + 256], CONTRACT_LAST)
                for s in range(2)
            ],
            axis=0,
        )
        for first in (0, 256, 512):
            width = min(256, 640 - first)
            block = terms[:, first : first + width]
            high = block.astype(BF16)
            low = (block - high.astype(F32)).astype(BF16)
            part = table[0:width, 0:width]
            rotated = dot(low, part) + dot(high, part)
            for i, k in enumerate(matrices):
                scale = scale_ref[k : k + 1, 0:1]
                total = None
                for start in (i * 128, height + i * 128):
                    scaled = jnp.clip(rotated[start : start + 128] * scale, -127.0, 127.0)
                    quantized = scaled.astype(BF16).astype(F32)
                    total = quantized if total is None else total + quantized
                for b in range(first // 128, (first + width) // 128):
                    half = total[:, b * 128 - first : b * 128 - first + 128].reshape(8, 2, 8, 128)
                    if b < 4:
                        term_ref[k * 8 + b] = half[:, 0].reshape(64, 128).astype(BF16)
                        term_ref[k * 8 + 4 + b] = half[:, 1].reshape(64, 128).astype(BF16)
                    else:
                        chosen = jnp.where(odd == 1, half[:, 1], half[:, 0])
                        term_ref[24 + k] = chosen.reshape(64, 128).astype(BF16)
                if first < 512:
                    send(k * 8 + first // 128, 2)
                    send(k * 8 + 4 + first // 128, 2)
                elif k == 1:
                    send(24, 8)
    for copy in copies:
        copy.wait()


def resid_kernel(acts_ref, w_ref, xa_ref, inv_ref, gain_ref, _, near_ref, far_ref):
    _, odd, first = places()
    gain = feature_column(gain_ref, first, odd)
    inverse = inv_ref[0:1, :]
    tails = acts_ref[0, 96:104, :].astype(F32)
    for x in range(1, 4):
        tails = tails + acts_ref[x, 96:104, :].astype(F32)
    row_mean = tails[0:1] + tails[1:2] + tails[2:3]
    pair = jnp.concatenate([gathered_acts(acts_ref, k) for k in range(2)], axis=0)
    normed_grad = dot(w_ref[0:256], pair, CONTRACT_FIRST)
    unit = xa_ref[...].astype(F32) * inverse
    resid = inverse * (normed_grad * gain - unit * row_mean)
    main, half = own_rows(odd)
    shared_half = jnp.where(odd == 1, resid[576:640], resid[512:576])
    near_ref[main, :] = resid[0:512, 0:256]
    near_ref[half, :] = shared_half[:, 0:256]
    far_ref[main, :] = resid[0:512, 256:512].astype(BF16)
    far_ref[half, :] = shared_half[:, 256:512].astype(BF16)


def finish_kernel(g_ref, near_ref, far_ref, out_ref, done_ref):
    out_ref[...] = (g_ref[...].astype(F32) + (near_ref[...] + far_ref[...].astype(F32))).astype(BF16)
    done_ref[...] = jnp.zeros((8, 128), F32)


def total_kernel(terms_ref, _, share_ref):
    totals = []
    for yh in range(2):
        total = terms_ref[yh].astype(F32)
        for i in range(1, 32):
            total = total + terms_ref[2 * i + yh].astype(F32)
        totals.append(total)
    for x in range(4):
        both = jnp.concatenate([total[x * 8 : x * 8 + 8] for total in totals], axis=0).astype(BF16)
        for i in range(32):
            share_ref[i * 4 + x] = both


def received_rows(m):
    start = 8 * (2 * (m % 4) + m // 4)
    return slice(start, start + 8)


def restore_kernel(both_ref, sign_ref, table_ref, scale_ref, out_ref, held, sems):
    table = table_ref[0:128, 0:128]
    copies = []
    for k in range(3):
        factor = scale_ref[3 + k : 4 + k, :]
        for q in range(2):

            def put(block, low_half, high_half):
                sign = (2 * sign_ref[block : block + 1, :] - 1).astype(F32) * factor
                both = jnp.concatenate([low_half, high_half], axis=0) * sign
                held[k, 16 * q : 16 * q + 16, block * 128 : (block + 1) * 128] = both.astype(BF16)

            own = dot(both_ref[q, k * 8 : k * 8 + 8].reshape(512, 128), table)
            for b in range(4):
                halves = [own[(4 * i + b) * 64 : (4 * i + b) * 64 + 64] for i in range(2)]
                for m in range(8):
                    rows = received_rows(m)
                    put(9 * (m // 2) + 5 * (m % 2) + b, halves[0][rows], halves[1][rows])
            shared = dot(both_ref[q, 24 + k], table)
            for p in range(4):
                put(9 * p + 4, shared[received_rows(2 * p)], shared[received_rows(2 * p + 1)])
        copy = pltpu.make_async_copy(held.at[k], out_ref.at[k], sems.at[k])
        copy.start()
        copies.append(copy)
    for copy in copies:
        copy.wait()


def call(kernel, outs, scalars=0, scratch=(), anywhere=(), out_space=pltpu.VMEM, limit=VMEM_LIMIT):
    def run(*operands):
        count = len(operands)
        spaces = [
            pltpu.SMEM if i >= count - scalars else pl.ANY if i in anywhere else pltpu.VMEM for i in range(count)
        ]
        return pl.pallas_call(
            kernel,
            out_shape=[jax.ShapeDtypeStruct(shape, dtype) for shape, dtype in outs],
            in_specs=[pl.BlockSpec(memory_space=place) for place in spaces],
            out_specs=[pl.BlockSpec(memory_space=out_space) for _ in outs],
            scratch_shapes=list(scratch),
            compiler_params=pltpu.CompilerParams(vmem_limit_bytes=limit),
            cost_estimate=pl.CostEstimate(flops=10**9, bytes_accessed=10**6, transcendentals=0),
            name=kernel.__name__,
        )(*operands)

    return run


def per_device(residual, out_grad, ffn_weights, norm_gain, exponents, sign_bits):
    gain = norm_gain.reshape(36, 128)
    signs = sign_bits.reshape(36, 128)
    table = jnp.asarray(np.kron(np.eye(2), signed_hadamard()), BF16)
    cores = [(0, 1), (1, 0)]
    x_cols, g_cols = residual.T, out_grad.T
    rows = ((640, 512), BF16)

    (send,) = call(
        prepare_kernel,
        [((8, 14, 16, 128), BF16)],
        scratch=[
            pltpu.VMEM((4, 3, 16, 1152), BF16),
            pltpu.VMEM((8, 14, 16, 128), BF16),
            pltpu.SemaphoreType.DMA((4,)),
            pltpu.SemaphoreType.DMA((8,)),
        ],
        anywhere=(0,),
        out_space=pl.ANY,
        limit=60 * 1024 * 1024,
    )(ffn_weights)
    received = lax.all_to_all(send.reshape(8, 224, 128), AXES, 0, 0, axis_index_groups=near_groups())
    near_x, near_g, _ = lax.optimization_barrier((x_cols, g_cols, send))
    (near,) = call(join_kernel, [((1152, 256), BF16)])(near_x, near_g)
    far = lax.ppermute(near, "c", cores)
    xa, ga, half, tail, scales = call(
        align_kernel, [rows, rows, ((128, 512), BF16), ((8, 512), BF16), ((8, 128), F32)], scalars=1
    )(near, far, exponents)
    other_half = lax.ppermute(half, "x", [(0, 1), (1, 0), (2, 3), (3, 2)])
    parts, mine, weights = call(
        forward_kernel, [((4, 104, 512), BF16), ((96, 512), F32), ((384, 640), BF16)], anywhere=(5,)
    )(
        received.reshape(8, 14, 16, 128), xa, ga, tail, gain, other_half
    )

    parts = lax.all_to_all(parts, "x", 0, 0)
    sums, own = call(sum_kernel, [((104, 512), BF16), ((96, 512), F32)])(parts, mine)
    sums = lax.all_gather(sums, "yh", axis=0)
    message, inverse = call(activation_kernel, [((4, 104, 512), BF16), ((8, 512), F32)])(sums, own)
    acts = lax.all_to_all(message, "x", 0, 0)
    (terms,) = call(
        gradient_kernel,
        [((32, 64, 128), BF16)],
        scratch=[pltpu.VMEM((32, 64, 128), BF16), pltpu.SemaphoreType.DMA((13,))],
        out_space=pl.ANY,
    )(acts, xa, ga, other_half, inverse, gain, signs, table, scales)

    summands = lax.all_to_all(terms.reshape(64, 32, 128), ("z", "yl", "yh"), 0, 0)
    near_resid, far_resid = call(resid_kernel, [((576, 256), F32), ((576, 256), BF16)], anywhere=(5,))(
        acts, weights, xa, inverse, gain, terms
    )
    far_resid = lax.ppermute(far_resid, "c", cores)
    resid_cols, done = call(finish_kernel, [((576, 256), BF16), ((8, 128), F32)])(g_cols, near_resid, far_resid)
    (share,) = call(total_kernel, [((128, 16, 128), BF16)])(summands, done)
    share = lax.all_to_all(share, ("z", "yl", "x"), 0, 0).reshape(32, 64, 128)
    both = lax.all_gather(share[0:27], "c", axis=0)
    (weight_grads,) = call(
        restore_kernel,
        [((3, 32, 4608), BF16)],
        scratch=[pltpu.VMEM((3, 32, 4608), BF16), pltpu.SemaphoreType.DMA((3,))],
        out_space=pl.ANY,
    )(both, signs, table, scales)
    return (resid_cols.T, weight_grads)


def near_groups():
    def flat(z, yl, c, yh, x):
        return (((z * 4 + yl) * 2 + c) * 2 + yh) * 4 + x

    return [
        [flat(z, 3 - yl if yh else yl, c, yh, x) for yh in range(2) for x in range(4)]
        for z in range(8)
        for yl in range(4)
        for c in range(2)
    ]


def solution(mesh):
    fine = Mesh(mesh.devices.reshape(8, 4, 2, 2, 4), AXES)
    rows = P(DP, MP)
    return jax.shard_map(
        per_device,
        mesh=fine,
        in_specs=(rows, rows, P(None, MP, None), P(), P(), P()),
        out_specs=(rows, P(None, MP, None)),
        check_vma=False,
    )
```

```python
import functools

import jax
import jax.numpy as jnp
import numpy as np
from jax import lax
from jax.experimental import pallas as pl
from jax.experimental.pallas import tpu as pltpu
from jax.sharding import Mesh
from jax.sharding import PartitionSpec as P

F32 = jnp.float32
BF16 = jnp.bfloat16
AXES = ("z", "yl", "c", "yh", "x")
DP = ("z", "yl", "c")
MP = ("yh", "x")
VMEM_LIMIT = 20 * 1024 * 1024
FEATURES = 4608
CONTRACT_LAST = (((1,), (1,)), ((), ()))
CONTRACT_FIRST = (((0,), (0,)), ((), ()))


def signed_hadamard():
    table = np.array([[1.0]], np.float32)
    for _ in range(7):
        table = np.block([[table, table], [table, -table]])
    return table


def gelu_parts(values):
    tanh_input = 0.7978845608 * (values + 0.044715 * values * values * values)
    tanhed = jnp.tanh(tanh_input)
    forward = 0.5 * values * (1.0 + tanhed)
    gelu_slope = 0.5 * (1.0 + tanhed) + 0.5 * values * (1.0 - tanhed * tanhed) * 0.7978845608 * (
        1.0 + 3.0 * 0.044715 * values * values
    )
    return (forward, gelu_slope)


def pieces(values):
    high = values.astype(BF16)
    rest = values - high.astype(F32)
    middle = rest.astype(BF16)
    low = (rest - middle.astype(F32)).astype(BF16)
    return (high, middle, low)


def dot(left, right, dims=(((1,), (0,)), ((), ()))):
    return lax.dot_general(left, right, dims, preferred_element_type=F32)


def places():
    odd = lax.axis_index("x") % 2
    pair = lax.axis_index("yh") * 2 + lax.axis_index("x") // 2
    return (lax.axis_index("c"), odd, pair * 9)


def local_rows(table_ref, first, odd):
    return [table_ref[pl.ds(first + 5 * odd + b, 1), :] for b in range(4)] + [table_ref[pl.ds(first + 4, 1), :]]


def own_rows(odd):
    return (
        pl.ds(pl.multiple_of(odd * 64, 64), 512),
        pl.ds(pl.multiple_of((1 - odd) * 512, 64), 64),
    )


def prepare_kernel(w_ref, send_ref, held, packed, in_sems, out_sems):
    core, _, _ = places()
    rows = pl.ds(pl.multiple_of(core * 16, 16), 16)
    loads = [
        pltpu.make_async_copy(w_ref.at[:, rows, pl.ds(p * 1152, 1152)], held.at[p], in_sems.at[p]) for p in range(4)
    ]
    for load in loads:
        load.start()
    lane = lax.broadcasted_iota(jnp.int32, (16, 128), 1)
    stores = []
    for m in range(8):
        pair, odd = m // 2, m % 2
        if odd == 0:
            loads[pair].wait()
        for b in range(4):
            column = (5 * odd + b) * 128
            for k in range(3):
                packed[m, b * 3 + k] = held[pair, k, :, column : column + 128]
        gate, up, down = [held[pair, k, :, 512:640] for k in range(3)]
        turned = pltpu.roll(up.astype(F32), 64, 1)
        packed[m, 12] = jnp.where((lane >= 64) == (odd == 1), gate.astype(F32), turned).astype(BF16)
        packed[m, 13] = down
        store = pltpu.make_async_copy(packed.at[m], send_ref.at[m], out_sems.at[m])
        store.start()
        stores.append(store)
    for store in stores:
        store.wait()


def join_kernel(x_ref, g_ref, out_ref):
    out_ref[0:576, :] = x_ref[...]
    out_ref[576:1152, :] = g_ref[...]


def align_kernel(near_ref, far_ref, exps_ref, xa_ref, ga_ref, half_ref, tail_ref, scale_ref):
    place = lax.broadcasted_iota(jnp.int32, (8, 128), 0)
    scales = jnp.zeros((8, 128), F32)
    for k in range(3):
        e = exps_ref[k]
        up = jnp.where(e == 3, 8.0, jnp.where(e == 4, 16.0, jnp.where(e == 5, 32.0, 64.0)))
        down = jnp.where(e == 3, 2.0**-9, jnp.where(e == 4, 2.0**-10, jnp.where(e == 5, 2.0**-11, 2.0**-12)))
        scales = jnp.where(place == k, up, jnp.where(place == 3 + k, down, scales))
    scale_ref[...] = scales * float(128.0**-0.5)
    _, odd, _ = places()
    main, half = pl.multiple_of(odd * 64, 64), pl.multiple_of((1 - odd) * 512, 64)
    mine = pl.ds(pl.multiple_of(512 + odd * 64, 64), 64)
    theirs = pl.ds(pl.multiple_of(576 - odd * 64, 64), 64)
    for part, to_ref in enumerate((xa_ref, ga_ref)):
        for side, ref in enumerate((near_ref, far_ref)):
            tokens = pl.ds(side * 256, 256)
            to_ref[0:512, tokens] = ref[pl.ds(576 * part + main, 512), :]
            rows = ref[pl.ds(576 * part + half, 64), :]
            half_ref[pl.ds(64 * part, 64), tokens] = rows
            to_ref[mine, tokens] = rows
            to_ref[theirs, tokens] = jnp.zeros((64, 256), BF16)
    wide = xa_ref[...].astype(F32)
    tail_ref[...] = stacked_pieces(jnp.sum(wide * wide, axis=0, keepdims=True))


def forward_kernel(recv_ref, xa_ref, ga_ref, tail_ref, gain_ref, _, part_ref, own_ref, w_ref):
    _, odd, first = places()
    for j in range(8):
        for k in range(3):
            rows = slice(k * 128 + j * 16, k * 128 + j * 16 + 16)
            for b in range(4):
                w_ref[rows, b * 128 : (b + 1) * 128] = recv_ref[j, b * 3 + k]
        w_ref[j * 16 : j * 16 + 16, 512:640] = recv_ref[j, 12]
        w_ref[128 + j * 16 : 128 + j * 16 + 16, 512:640] = pltpu.roll(recv_ref[j, 12].astype(F32), 64, 1).astype(BF16)
        w_ref[256 + j * 16 : 256 + j * 16 + 16, 512:640] = recv_ref[j, 13]
    gained = w_ref[0:256].astype(F32) * jnp.concatenate(local_rows(gain_ref, first, odd), axis=1)
    high = gained.astype(BF16)
    low = (gained - high.astype(F32)).astype(BF16)
    both = dot(jnp.concatenate([low, high], axis=0), xa_ref[...])
    gate_up = both[0:256] + both[256:512]
    down = dot(w_ref[256:384], ga_ref[...])
    tail = tail_ref[...]
    my_x = lax.axis_index("x")
    for yh in range(2):
        for k, source in enumerate((gate_up[0:128], gate_up[128:256], down)):
            rows = slice(yh * 48 + k * 16, yh * 48 + k * 16 + 16)
            own = jnp.zeros((16, 512), F32)
            for x in range(4):
                j = 4 * yh + x
                values = source[j * 16 : j * 16 + 16]
                part_ref[x, rows, :] = values.astype(BF16)
                own = jnp.where(my_x == x, values, own)
            own_ref[rows, :] = own
    for x in range(4):
        part_ref[x, 96:104, :] = tail


def stacked_pieces(row):
    place = lax.broadcasted_iota(jnp.int32, (8, 512), 0)
    tail = jnp.zeros((8, 512), F32)
    for i, piece in enumerate(pieces(row)):
        tail = jnp.where(place == i, piece.astype(F32), tail)
    return tail.astype(BF16)


def sum_kernel(parts_ref, mine_ref, out_ref, own_ref):
    my_x = lax.axis_index("x")
    total = mine_ref[...]
    tails = jnp.zeros((8, 512), F32)
    for i in range(4):
        total = total + jnp.where(my_x == i, 0.0, parts_ref[i, 0:96, :].astype(F32))
        tails = tails + parts_ref[i, 96:104, :].astype(F32)
    own_ref[...] = total
    out_ref[0:96, :] = total.astype(BF16)
    out_ref[96:104, :] = stacked_pieces(tails[0:1] + tails[1:2] + tails[2:3])


def activation_kernel(parts_ref, own_ref, out_ref, inv_ref):
    high = lax.axis_index("yh") == 1
    tails = parts_ref[0, 96:104, :].astype(F32) + parts_ref[1, 96:104, :].astype(F32)
    sums = tails[0:1] + tails[1:2] + tails[2:3]
    inverse = lax.rsqrt(sums / FEATURES + 1e-06)
    inv_ref[...] = jnp.broadcast_to(inverse, (8, 512))
    others = [parts_ref[i, 0:96, :].astype(F32) for i in range(2)]
    total = own_ref[...] + jnp.where(high, others[0], others[1])
    mean = jnp.zeros((1, 512), F32)
    for yh in range(2):
        start = yh * 48
        gate_pre = total[start : start + 16] * inverse
        up_proj = total[start + 16 : start + 32] * inverse
        hidden_grad = total[start + 32 : start + 48]
        activated, slope = gelu_parts(gate_pre)
        hidden = (activated * up_proj).astype(BF16)
        gate_grad = (hidden_grad * up_proj * slope).astype(BF16)
        up_grad = (hidden_grad * activated).astype(BF16)
        products = gate_grad.astype(F32) * gate_pre + up_grad.astype(F32) * up_proj
        mean = mean + jnp.sum(products, axis=0, keepdims=True) / FEATURES
        for i in range(4):
            out_ref[i, start : start + 16, :] = gate_grad
            out_ref[i, start + 16 : start + 32, :] = up_grad
            out_ref[i, start + 32 : start + 48, :] = hidden
    tail = stacked_pieces(mean)
    for i in range(4):
        out_ref[i, 96:104, :] = tail


def feature_column(table_ref, first, odd):
    diagonal = lax.broadcasted_iota(jnp.int32, (128, 128), 0) == lax.broadcasted_iota(jnp.int32, (128, 128), 1)
    rows = local_rows(table_ref, first, odd)
    return jnp.concatenate(
        [jnp.sum(jnp.where(diagonal, row.astype(F32), 0.0), axis=1, keepdims=True) for row in rows], axis=0
    )


def gathered_acts(acts_ref, k):
    starts = [(j % 4, j // 4 * 48 + k * 16) for j in range(8)]
    return jnp.concatenate([acts_ref[x, start : start + 16, :] for x, start in starts], axis=0)


def gradient_kernel(
    acts_ref, xa_ref, ga_ref, half_ref, inv_ref, gain_ref, sign_ref, table_ref, scale_ref, out_ref, term_ref, sems
):
    _, odd, first_block = places()
    table = table_ref[...]
    sign = 2.0 * feature_column(sign_ref, first_block, odd) - 1.0
    gain = feature_column(gain_ref, first_block, odd) * sign
    theirs = (lax.broadcasted_iota(jnp.int32, (128, 512), 0) >= 64) == (odd == 0)

    def right_of(part, ref, row, column):
        other = half_ref[part * 64 : part * 64 + 64, :].astype(F32)
        shared = jnp.where(theirs, jnp.concatenate([other, other], axis=0), ref[512:640, :].astype(F32))
        values = jnp.concatenate([ref[0:512, :].astype(F32), shared], axis=0)
        return ((values if row is None else values * row) * column).astype(BF16)

    for s in range(27, 32):
        term_ref[s] = jnp.zeros((64, 128), BF16)
    copies = []

    def send(at, count):
        copy = pltpu.make_async_copy(term_ref.at[pl.ds(at, count)], out_ref.at[pl.ds(at, count)], sems.at[len(copies)])
        copy.start()
        copies.append(copy)

    send(27, 5)
    for matrices in ((2,), (0, 1)):
        right = right_of(1, ga_ref, None, sign) if matrices == (2,) else right_of(0, xa_ref, inv_ref[0:1, :], gain)
        acts = jnp.concatenate([gathered_acts(acts_ref, k) for k in matrices], axis=0)
        height = acts.shape[0]
        terms = jnp.concatenate(
            [
                dot(acts[:, s * 256 : s * 256 + 256], right[:, s * 256 : s * 256 + 256], CONTRACT_LAST)
                for s in range(2)
            ],
            axis=0,
        )
        for first in (0, 256, 512):
            width = min(256, 640 - first)
            block = terms[:, first : first + width]
            high = block.astype(BF16)
            low = (block - high.astype(F32)).astype(BF16)
            part = table[0:width, 0:width]
            rotated = dot(low, part) + dot(high, part)
            for i, k in enumerate(matrices):
                scale = scale_ref[k : k + 1, 0:1]
                total = None
                for start in (i * 128, height + i * 128):
                    scaled = jnp.clip(rotated[start : start + 128] * scale, -127.0, 127.0)
                    quantized = scaled.astype(BF16).astype(F32)
                    total = quantized if total is None else total + quantized
                for b in range(first // 128, (first + width) // 128):
                    half = total[:, b * 128 - first : b * 128 - first + 128].reshape(8, 2, 8, 128)
                    if b < 4:
                        term_ref[k * 8 + b] = half[:, 0].reshape(64, 128).astype(BF16)
                        term_ref[k * 8 + 4 + b] = half[:, 1].reshape(64, 128).astype(BF16)
                    else:
                        chosen = jnp.where(odd == 1, half[:, 1], half[:, 0])
                        term_ref[24 + k] = chosen.reshape(64, 128).astype(BF16)
                if first < 512:
                    send(k * 8 + first // 128, 2)
                    send(k * 8 + 4 + first // 128, 2)
                elif k == 1:
                    send(24, 3)
    for copy in copies:
        copy.wait()


def resid_kernel(acts_ref, w_ref, xa_ref, inv_ref, gain_ref, _, near_ref, far_ref):
    _, odd, first = places()
    gain = feature_column(gain_ref, first, odd)
    inverse = inv_ref[0:1, :]
    tails = acts_ref[0, 96:104, :].astype(F32)
    for x in range(1, 4):
        tails = tails + acts_ref[x, 96:104, :].astype(F32)
    row_mean = tails[0:1] + tails[1:2] + tails[2:3]
    pair = jnp.concatenate([gathered_acts(acts_ref, k) for k in range(2)], axis=0)
    normed_grad = dot(w_ref[0:256], pair, CONTRACT_FIRST)
    unit = xa_ref[...].astype(F32) * inverse
    resid = inverse * (normed_grad * gain - unit * row_mean)
    main, half = own_rows(odd)
    shared_half = jnp.where(odd == 1, resid[576:640], resid[512:576])
    near_ref[main, :] = resid[0:512, 0:256]
    near_ref[half, :] = shared_half[:, 0:256]
    far_ref[main, :] = resid[0:512, 256:512].astype(BF16)
    far_ref[half, :] = shared_half[:, 256:512].astype(BF16)


def finish_kernel(g_ref, near_ref, far_ref, out_ref, done_ref):
    out_ref[...] = (g_ref[...].astype(F32) + (near_ref[...] + far_ref[...].astype(F32))).astype(BF16)
    done_ref[...] = jnp.zeros((8, 128), F32)


def total_kernel(terms_ref, _, share_ref):
    totals = []
    for yh in range(2):
        total = terms_ref[yh].astype(F32)
        for i in range(1, 32):
            total = total + terms_ref[2 * i + yh].astype(F32)
        totals.append(total)
    for x in range(4):
        both = jnp.concatenate([total[x * 8 : x * 8 + 8] for total in totals], axis=0).astype(BF16)
        for i in range(32):
            share_ref[i * 4 + x] = both


def received_rows(m):
    start = 8 * (2 * (m % 4) + m // 4)
    return slice(start, start + 8)


def restore_kernel(both_ref, sign_ref, table_ref, scale_ref, out_ref, held, sems):
    table = table_ref[0:128, 0:128]
    copies = []
    for k in range(3):
        factor = scale_ref[3 + k : 4 + k, :]
        for q in range(2):

            def put(block, low_half, high_half):
                sign = (2 * sign_ref[block : block + 1, :] - 1).astype(F32) * factor
                both = jnp.concatenate([low_half, high_half], axis=0) * sign
                held[k, 16 * q : 16 * q + 16, block * 128 : (block + 1) * 128] = both.astype(BF16)

            own = dot(both_ref[q, k * 8 : k * 8 + 8].reshape(512, 128), table)
            for b in range(4):
                halves = [own[(4 * i + b) * 64 : (4 * i + b) * 64 + 64] for i in range(2)]
                for m in range(8):
                    rows = received_rows(m)
                    put(9 * (m // 2) + 5 * (m % 2) + b, halves[0][rows], halves[1][rows])
            shared = dot(both_ref[q, 24 + k], table)
            for p in range(4):
                put(9 * p + 4, shared[received_rows(2 * p)], shared[received_rows(2 * p + 1)])
        copy = pltpu.make_async_copy(held.at[k], out_ref.at[k], sems.at[k])
        copy.start()
        copies.append(copy)
    for copy in copies:
        copy.wait()


def call(kernel, outs, scalars=0, scratch=(), anywhere=(), out_space=pltpu.VMEM, limit=VMEM_LIMIT):
    def run(*operands):
        count = len(operands)
        spaces = [
            pltpu.SMEM if i >= count - scalars else pl.ANY if i in anywhere else pltpu.VMEM for i in range(count)
        ]
        return pl.pallas_call(
            kernel,
            out_shape=[jax.ShapeDtypeStruct(shape, dtype) for shape, dtype in outs],
            in_specs=[pl.BlockSpec(memory_space=place) for place in spaces],
            out_specs=[pl.BlockSpec(memory_space=out_space) for _ in outs],
            scratch_shapes=list(scratch),
            compiler_params=pltpu.CompilerParams(vmem_limit_bytes=limit),
            cost_estimate=pl.CostEstimate(flops=10**9, bytes_accessed=10**6, transcendentals=0),
            name=kernel.__name__,
        )(*operands)

    return run


def per_device(residual, out_grad, ffn_weights, norm_gain, exponents, sign_bits):
    gain = norm_gain.reshape(36, 128)
    signs = sign_bits.reshape(36, 128)
    table = jnp.asarray(np.kron(np.eye(2), signed_hadamard()), BF16)
    cores = [(0, 1), (1, 0)]
    x_cols, g_cols = residual.T, out_grad.T
    rows = ((640, 512), BF16)

    (send,) = call(
        prepare_kernel,
        [((8, 14, 16, 128), BF16)],
        scratch=[
            pltpu.VMEM((4, 3, 16, 1152), BF16),
            pltpu.VMEM((8, 14, 16, 128), BF16),
            pltpu.SemaphoreType.DMA((4,)),
            pltpu.SemaphoreType.DMA((8,)),
        ],
        anywhere=(0,),
        out_space=pl.ANY,
        limit=60 * 1024 * 1024,
    )(ffn_weights)
    received = lax.all_to_all(send.reshape(8, 224, 128), AXES, 0, 0, axis_index_groups=near_groups())
    near_x, near_g, _ = lax.optimization_barrier((x_cols, g_cols, send))
    (near,) = call(join_kernel, [((1152, 256), BF16)])(near_x, near_g)
    far = lax.ppermute(near, "c", cores)
    xa, ga, half, tail, scales = call(
        align_kernel, [rows, rows, ((128, 512), BF16), ((8, 512), BF16), ((8, 128), F32)], scalars=1
    )(near, far, exponents)
    other_half = lax.ppermute(half, "x", [(0, 1), (1, 0), (2, 3), (3, 2)])
    parts, mine, weights = call(
        forward_kernel, [((4, 104, 512), BF16), ((96, 512), F32), ((384, 640), BF16)], anywhere=(5,)
    )(
        received.reshape(8, 14, 16, 128), xa, ga, tail, gain, other_half
    )

    parts = lax.all_to_all(parts, "x", 0, 0)
    sums, own = call(sum_kernel, [((104, 512), BF16), ((96, 512), F32)])(parts, mine)
    sums = lax.all_gather(sums, "yh", axis=0)
    message, inverse = call(activation_kernel, [((4, 104, 512), BF16), ((8, 512), F32)])(sums, own)
    acts = lax.all_to_all(message, "x", 0, 0)
    (terms,) = call(
        gradient_kernel,
        [((32, 64, 128), BF16)],
        scratch=[pltpu.VMEM((32, 64, 128), BF16), pltpu.SemaphoreType.DMA((14,))],
        out_space=pl.ANY,
    )(acts, xa, ga, other_half, inverse, gain, signs, table, scales)

    summands = lax.all_to_all(terms.reshape(64, 32, 128), ("z", "yl", "yh"), 0, 0)
    near_resid, far_resid = call(resid_kernel, [((576, 256), F32), ((576, 256), BF16)], anywhere=(5,))(
        acts, weights, xa, inverse, gain, terms
    )
    far_resid = lax.ppermute(far_resid, "c", cores)
    resid_cols, done = call(finish_kernel, [((576, 256), BF16), ((8, 128), F32)])(g_cols, near_resid, far_resid)
    (share,) = call(total_kernel, [((128, 16, 128), BF16)])(summands, done)
    share = lax.all_to_all(share, ("z", "yl", "x"), 0, 0).reshape(32, 64, 128)
    both = lax.all_gather(share[0:27], "c", axis=0)
    (weight_grads,) = call(
        restore_kernel,
        [((3, 32, 4608), BF16)],
        scratch=[pltpu.VMEM((3, 32, 4608), BF16), pltpu.SemaphoreType.DMA((3,))],
        out_space=pl.ANY,
    )(both, signs, table, scales)
    return (resid_cols.T, weight_grads)


def near_groups():
    def flat(z, yl, c, yh, x):
        return (((z * 4 + yl) * 2 + c) * 2 + yh) * 4 + x

    return [
        [flat(z, 3 - yl if yh else yl, c, yh, x) for yh in range(2) for x in range(4)]
        for z in range(8)
        for yl in range(4)
        for c in range(2)
    ]


def solution(mesh):
    fine = Mesh(mesh.devices.reshape(8, 4, 2, 2, 4), AXES)
    rows = P(DP, MP)
    return jax.shard_map(
        per_device,
        mesh=fine,
        in_specs=(rows, rows, P(None, MP, None), P(), P(), P()),
        out_specs=(rows, P(None, MP, None)),
        check_vma=False,
    )
```
